128 devices in a mesh: replica: 4 (over y_lo, core), fsdp: 32 (over y_hi, z, x).
Axes of the slice: x: 4, y: 4 (y_hi: 2, y_lo: 2; y = y_hi * 2 + y_lo), z: 4, core: 2. Of those that a mesh axis runs over, the one named last changes fastest.
Arguments:
- inputs: bfloat16 [4, 16384, 1536], P('replica', 'fsdp'), may hold values from -6 to 6
- token_ids: int32 [4, 16384], P('replica', 'fsdp'), may hold values from 0 to 32063, as said below
- upstream: bfloat16 [4, 16384, 6144], P('replica', 'fsdp'), may hold values from -0.119628906 to 0.119628906
- weight: bfloat16 [4, 1536, 6144], P('replica', 'fsdp'), may hold values from -0.15625 to 0.15625
- frag_index: int32 [16], replicated, may hold values from 0 to 15, each once
- global_params: float32 [16, 2097152], P(None, 'fsdp'), may hold values from -6 to 6
- local_params: float32 [4, 16, 2097152], P('replica', None, 'fsdp'), may hold values from -6 to 6
- momentum: float32 [16, 2097152], P(None, 'fsdp'), may hold values from -3 to 3
Outputs:
- weight_grad: bfloat16 [4, 1536, 6144], P('replica', 'fsdp')
- new_global: float32 [2097152], P('fsdp')
- new_momentum: float32 [2097152], P('fsdp')
The draws below stay inside these ranges and needn't reach their ends.
Inputs may be any that keep to these rules, and one draw needn't show every extreme that they name: `token_ids`: within each aligned block of 512 tokens of a replica, padding (id 0) forms a tail of 0 to 256 tokens; other ids are 1 or more.
All inputs are finite; a program needn't handle non-finite values.
Results may differ from the reference program's by a relative error of at most 0.029.
Values may be sent and summed in bfloat16 or wider, within the bound.
A program may use at most 128 MiB of HBM per device.

```python
import jax
import jax.numpy as jnp
from jax import lax

DW = 1536
FW = 6144
VOCAB = 32064
TOK_DEV = 512
NFRAG = 16
TOKENS = 16384
FRAG = 2097152
N_REPLICA = 4
N_FSDP = 32


def draw_token_ids(key, part):
    key = jax.random.fold_in(key, 11)
    id_key, pad_key = jax.random.split(key)
    values = jax.random.randint(id_key, (N_REPLICA, N_FSDP, TOK_DEV), 1, VOCAB)
    padding = jax.random.randint(pad_key, (N_REPLICA, N_FSDP, 1), 0, TOK_DEV // 2 + 1)
    position = jnp.arange(TOK_DEV, dtype=jnp.int32)[None, None, :]
    values = jnp.where(position < TOK_DEV - padding, values, 0)
    return values.reshape(N_REPLICA, TOKENS).astype(jnp.int32)


def spiked(values, own_key, source, target, parts, factor):
    owner, partner = [(jnp.arange(values.shape[dim]) // (values.shape[dim] // parts)).reshape([-1 if axis == dim else 1 for axis in range(values.ndim)]) for dim in (source, target)]
    chosen = jax.random.permutation(own_key, parts)[partner]
    strong = (owner == chosen) | (owner == (partner + parts // 2) % parts)
    return jnp.where(strong, factor * values, values)


def levels(rng, shape, cuts, smallest, largest):
    gain, own = 1.0, jax.random.fold_in(rng, 6)
    for dim, blocks in cuts:
        steps = jnp.exp(jax.random.uniform(jax.random.fold_in(own, dim), (blocks,), jnp.float32, smallest / len(cuts), largest / len(cuts)))
        gain = gain * jnp.repeat(steps, shape[dim] // blocks).reshape([-1 if axis == dim else 1 for axis in range(len(shape))])
    return gain


def bell_draw(rng, shape, width, most, shards=(), held_as=jnp.bfloat16):
    drawn = width * jax.random.normal(rng, shape, jnp.float32)
    if shards:
        drawn = drawn * levels(rng, shape, shards, -0.22, 0.18)
    return jnp.clip(drawn, -most, most).astype(held_as)


def noise_with(key, extent, deviation, bound, cuts, heavy, kind=jnp.bfloat16):
    result = deviation * jax.random.normal(key, extent, jnp.float32)
    if cuts:
        result = result * levels(key, extent, cuts, -0.22, 0.18)
    return jnp.clip(spiked(result, jax.random.fold_in(key, 3), *heavy), -bound, bound).astype(kind)


def setup_inputs(seed: int = 0) -> dict:
    key_of = jax.random.split(jax.random.key(seed), 9)
    inputs = noise_with(key_of[0], (N_REPLICA, TOKENS, DW), 1.0, 6.0, ((0, 4), (1, 32)), (1, 2, 32, 2.75))
    token_ids = draw_token_ids(jax.random.fold_in(key_of[8], 71), 0)
    upstream = bell_draw(key_of[2], (N_REPLICA, TOKENS, FW), 0.02, 0.119628906, ((0, 4), (1, 32)))
    weight = bell_draw(key_of[3], (N_REPLICA, DW, FW), DW ** -0.5, 0.15625, ((0, 4), (1, 32)))
    frag_index = jax.random.permutation(key_of[4], NFRAG).astype(jnp.int32)
    global_params = bell_draw(key_of[5], (NFRAG, FRAG), 1.0, 6.0, ((1, 32),), jnp.float32)
    local_params = bell_draw(key_of[6], (N_REPLICA, NFRAG, FRAG), 1.0, 6.0, ((0, 4), (2, 32)), jnp.float32)
    momentum = bell_draw(key_of[7], (NFRAG, FRAG), 0.5, 3.0, ((1, 32),), jnp.float32)
    return {"inputs": inputs, "token_ids": token_ids, "upstream": upstream, "weight": weight, "frag_index": frag_index, "global_params": global_params, "local_params": local_params, "momentum": momentum}


def replica_grad(packed):
    inputs, token_ids, upstream, weight = packed
    pre = jnp.dot(inputs, weight, preferred_element_type=jnp.float32)
    sig = jax.nn.sigmoid(pre)
    deriv = sig * (1.0 + pre * (1.0 - sig))
    keep = (token_ids != 0).astype(jnp.float32)[:, None]
    eff = (keep * upstream.astype(jnp.float32) * deriv).astype(jnp.bfloat16)
    in_blocks = inputs.reshape(N_FSDP, TOK_DEV, DW)
    eff_blocks = eff.reshape(N_FSDP, TOK_DEV, FW)

    def accumulate(total, block):
        part = lax.dot_general(block[0], block[1], (((0,), (0,)), ((), ())), preferred_element_type=jnp.float32)
        part = lax.optimization_barrier(part.astype(jnp.bfloat16))
        return (total + part.astype(jnp.float32), None)
    total, unused = lax.scan(accumulate, jnp.zeros((DW, FW), jnp.float32), (in_blocks, eff_blocks))
    return total.astype(jnp.bfloat16)

def reference(inputs, token_ids, upstream, weight, frag_index, global_params, local_params, momentum):
    weight_grad = lax.map(replica_grad, (inputs, token_ids, upstream, weight))
    fragment = frag_index[0]
    chosen = lax.dynamic_index_in_dim(global_params, fragment, 0, keepdims=False)
    local_now = lax.dynamic_index_in_dim(local_params, fragment, 1, keepdims=False)
    moment_now = lax.dynamic_index_in_dim(momentum, fragment, 0, keepdims=False)
    delta = lax.optimization_barrier(jnp.sum(chosen[None, :] - local_now, axis=0)) / N_REPLICA
    new_momentum = 0.9 * moment_now + delta
    new_global = chosen - 0.7 * (delta + 0.9 * new_momentum)
    return (weight_grad, new_global, new_momentum)
```

```python
import functools

import jax
import jax.numpy as jnp
from jax import lax
from jax.experimental import pallas as pl
from jax.experimental.pallas import tpu as pltpu
from jax.sharding import PartitionSpec as P

MESH = pl.DeviceIdType.MESH
TOK, DW, FW = 512, 1536, 6144
ROWS = 48
HALF = 768
COLS = 1536
CHUNKS = ((0, 256), (256, 512), (768, 512), (1280, 256))
FIRST = ((0, 256), (256, 1280))
DIST = (1, 3, 2)
MB = 256


def kernel(
    x_hbm, ids_ref, up_hbm, w_hbm, out_hbm,
    X, XT, U, W, E, G, RY, RX, T, K,
    own_sem, a_s, a_r, k_s, k_r, x_s, x_r, u_s, u_r,
    b_s, b_r, c_s, c_r, d_s, d_r, e_s, e_r, f_s, f_r,
):
    core = lax.rem(lax.axis_index("replica"), 2)
    me = lax.axis_index("fsdp")
    h, z, x = lax.div(me, 16), lax.rem(lax.div(me, 4), 4), lax.rem(me, 4)
    p = z + core * (x - z)
    q = x + core * (z - x)

    def place(hh, pp, qq):
        return hh * 16 + (pp + core * (qq - pp)) * 4 + (qq + core * (pp - qq))

    def rows(hh, pp, qq):
        return pl.ds(pl.multiple_of(place(hh, pp, qq) * ROWS, 16), ROWS)

    def ahead(a, d):
        return lax.rem(a + d, 4)

    def remote(src, dst, send, recv, device):
        return pltpu.make_async_remote_copy(
            src_ref=src, dst_ref=dst, send_sem=send, recv_sem=recv,
            device_id={"fsdp": device}, device_id_type=MESH,
        )

    sent = []

    def quarter(pp, c0, cw):
        return pl.ds(pl.multiple_of(pp * COLS + c0, 128), cw)

    barrier = pltpu.get_barrier_semaphore()
    near = [place(h, ahead(p, d), q) for d in DIST]
    side = [place(h, p, ahead(q, d)) for d in DIST]
    over = place(1 - h, p, q)
    for device in near + side + [over]:
        pl.semaphore_signal(barrier, inc=1, device_id={"fsdp": device}, device_id_type=MESH)
    pl.semaphore_wait(barrier, 7)

    own = []
    weight_in = []
    for n, (c0, cw) in enumerate(FIRST):
        place_w = W.at[rows(h, p, q), pl.ds(c0, cw)]
        copies = []
        for i, d in enumerate(DIST):
            copy = remote(
                w_hbm.at[0, :, quarter(ahead(p, d), c0, cw)], place_w,
                a_s.at[n, i], a_r.at[n, i], near[i],
            )
            copy.start()
            copies.append(copy)
        mine = pltpu.make_async_copy(w_hbm.at[0, :, quarter(p, c0, cw)], place_w, own_sem.at[n])
        mine.start()
        weight_in.append((mine, copies))
        sent += copies

    K[p] = jnp.broadcast_to((ids_ref[...] != 0).astype(jnp.float32), (8, TOK))
    x_in, k_in = [], []
    for i in range(3):
        k_in.append(remote(K.at[p], K.at[p], k_s.at[i], k_r.at[i], near[i]))
        k_in[i].start()
    for i in range(3):
        x_in.append(remote(x_hbm.at[0], X.at[p], x_s.at[i], x_r.at[i], near[i]))
        x_in[i].start()
    x_own = pltpu.make_async_copy(x_hbm.at[0], X.at[p], own_sem.at[2])
    x_own.start()
    u_in = []
    for n, (c0, cw) in enumerate(CHUNKS):
        there = U.at[p, :, pl.ds(c0, cw)]
        copies = []
        for i, d in enumerate(DIST):
            copy = remote(
                up_hbm.at[0, :, quarter(ahead(p, d), c0, cw)], there,
                u_s.at[n, i], u_r.at[n, i], near[i],
            )
            copy.start()
            copies.append(copy)
        u_in.append(copies)
        sent += copies
    u_own = pltpu.make_async_copy(up_hbm.at[0, :, quarter(p, 0, COLS)], U.at[p], own_sem.at[3])
    u_own.start()
    sent += x_in + k_in

    def arrive(copies):
        for copy in copies:
            copy.wait_recv()

    side_in = []

    def to_side(n):
        c0, cw = CHUNKS[n]
        cols = pl.ds(c0, cw)
        totals = []
        for i in range(3):
            for pp in range(4):
                part = W.at[rows(h, pp, q), cols]
                remote(part, part, b_s.at[n, i], b_r.at[n, i], side[i]).start()
            whole = W.at[pl.ds(0, 4 * ROWS), cols]
            totals.append(remote(whole, whole, b_s.at[n, i], b_r.at[n, i], side[i]))
        side_in.append(totals)
        sent.extend(totals)

    over_in = []

    def to_over(n):
        arrive(side_in[n])
        c0, cw = CHUNKS[n]
        half = W.at[pl.ds(pl.multiple_of(h * HALF, 16), HALF), pl.ds(c0, cw)]
        copy = remote(half, half, c_s.at[n], c_r.at[n], over)
        copy.start()
        over_in.append(copy)
        sent.append(copy)

    def turn(t):
        kept = K[t][0:1, :].astype(jnp.bfloat16)

        def step(j, carry):
            cols = pl.ds(pl.multiple_of(j * 256, 256), 256)
            XT[t, cols, :] = jnp.transpose(X[t, :, cols]) * kept
            return carry

        lax.fori_loop(0, DW // 256, step, 0)

    weight_in[0][0].wait()
    arrive(weight_in[0][1])
    to_side(0)
    weight_in[1][0].wait()
    arrive(weight_in[1][1])
    for n in range(1, len(CHUNKS)):
        to_side(n)
    to_over(0)
    x_own.wait()
    turn(p)
    for n in range(1, len(CHUNKS)):
        to_over(n)
    u_own.wait()
    blocks = [p] + [lax.rem(p - d + 4, 4) for d in DIST]
    for i in range(3):
        k_in[i].wait_recv()
        x_in[i].wait_recv()
        turn(blocks[i + 1])

    def forward(n, t):
        c0, cw = CHUNKS[n]

        def step(m, carry):
            part = pl.ds(pl.multiple_of(m * MB, MB), MB)
            pre = jnp.dot(X[t, part, :], W[:, c0 : c0 + cw], preferred_element_type=jnp.float32)
            sig = jax.nn.sigmoid(pre)
            deriv = sig * (1.0 + pre * (1.0 - sig))
            eff = U[t, part, c0 : c0 + cw].astype(jnp.float32) * deriv
            E[t, part, 0:cw] = eff.astype(jnp.bfloat16)
            return carry

        lax.fori_loop(0, TOK // MB, step, 0)

    def grad(n, half):
        c0, cw = CHUNKS[n]

        def step(m, carry):
            part = pl.ds(pl.multiple_of(half * HALF + m * 256, 256), 256)
            acc = jnp.dot(XT[0, part, :], E[0, :, 0:cw], preferred_element_type=jnp.float32)
            for t in range(1, 4):
                acc += jnp.dot(XT[t, part, :], E[t, :, 0:cw], preferred_element_type=jnp.float32)
            G[part, c0 : c0 + cw] = acc.astype(jnp.bfloat16)
            return carry

        lax.fori_loop(0, HALF // 256, step, 0)

    back_in = []

    def compute(n):
        c0, cw = CHUNKS[n]
        over_in[n].wait_recv()
        forward(n, blocks[0])
        for i in range(3):
            u_in[n][i].wait_recv()
            forward(n, blocks[i + 1])
        grad(n, 1 - h)
        copy = remote(
            G.at[pl.ds(pl.multiple_of((1 - h) * HALF, 16), HALF), pl.ds(c0, cw)],
            RY.at[:, pl.ds(c0, cw)], d_s.at[n], d_r.at[n], over,
        )
        copy.start()
        back_in.append(copy)
        sent.append(copy)
        grad(n, h)

    sums_in = []

    def reduce_over(n):
        c0, cw = CHUNKS[n]
        back_in[n].wait_recv()

        def step(m, carry):
            here = pl.ds(pl.multiple_of(h * HALF + m * 64, 64), 64)
            there = pl.ds(pl.multiple_of(m * 64, 64), 64)
            total = G[here, c0 : c0 + cw].astype(jnp.float32) + RY[there, c0 : c0 + cw].astype(jnp.float32)
            G[here, c0 : c0 + cw] = total.astype(jnp.bfloat16)
            return carry

        lax.fori_loop(0, HALF // 64, step, 0)
        totals = []
        for i, d in enumerate(DIST):
            for pp in range(4):
                remote(
                    G.at[rows(h, pp, ahead(q, d)), pl.ds(c0, cw)],
                    RX.at[i, pl.ds(pp * ROWS, ROWS), pl.ds(c0, cw)],
                    e_s.at[n, i], e_r.at[n, i], side[i],
                ).start()
            whole = RX.at[i, :, pl.ds(c0, cw)]
            totals.append(remote(whole, whole, e_s.at[n, i], e_r.at[n, i], side[i]))
        sums_in.append(totals)
        sent.extend(totals)

    last_in = []

    def reduce_side(n):
        c0, cw = CHUNKS[n]
        arrive(sums_in[n])

        def step(pp, carry):
            part = pl.ds(pl.multiple_of(pp * ROWS, 16), ROWS)
            total = G[rows(h, pp, q), c0 : c0 + cw].astype(jnp.float32)
            for i in range(3):
                total += RX[i, part, c0 : c0 + cw].astype(jnp.float32)
            T[part, c0 : c0 + cw] = total.astype(jnp.bfloat16)
            return carry

        lax.fori_loop(0, 4, step, 0)
        there = out_hbm.at[0, :, quarter(p, c0, cw)]
        copies = []
        for i, d in enumerate(DIST):
            part = pl.ds(pl.multiple_of(ahead(p, d) * ROWS, 16), ROWS)
            copy = remote(T.at[part, pl.ds(c0, cw)], there, f_s.at[n, i], f_r.at[n, i], near[i])
            copy.start()
            copies.append(copy)
        part = pl.ds(pl.multiple_of(p * ROWS, 16), ROWS)
        mine = pltpu.make_async_copy(T.at[part, pl.ds(c0, cw)], there, own_sem.at[4 + n])
        mine.start()
        own.append(mine)
        last_in.append(copies)
        sent.extend(copies)

    compute(0)
    compute(1)
    compute(2)
    reduce_over(0)
    compute(3)
    reduce_over(1)
    reduce_side(0)
    reduce_over(2)
    reduce_side(1)
    reduce_over(3)
    reduce_side(2)
    reduce_side(3)
    for copies in last_in:
        arrive(copies)
    for mine in own:
        mine.wait()
    for copy in sent:
        copy.wait_send()


def inner_grad(inputs, token_ids, upstream, weight):
    n = len(CHUNKS)
    bf16 = jnp.bfloat16
    sems = [pltpu.SemaphoreType.DMA((4 + n,))]
    for shape in ((2, 3), (3,), (3,), (n, 3), (n, 3), (n,), (n,), (n, 3), (n, 3)):
        sems += [pltpu.SemaphoreType.DMA(shape)] * 2
    hbm = pl.BlockSpec(memory_space=pl.ANY)
    return pl.pallas_call(
        kernel,
        name="inner_grad",
        out_shape=jax.ShapeDtypeStruct((1, ROWS, FW), bf16),
        in_specs=[hbm, pl.BlockSpec(memory_space=pltpu.VMEM), hbm, hbm],
        out_specs=hbm,
        scratch_shapes=[
            pltpu.VMEM((4, TOK, DW), bf16),
            pltpu.VMEM((4, DW, TOK), bf16),
            pltpu.VMEM((4, TOK, COLS), bf16),
            pltpu.VMEM((DW, COLS), bf16),
            pltpu.VMEM((4, TOK, 512), bf16),
            pltpu.VMEM((DW, COLS), bf16),
            pltpu.VMEM((HALF, COLS), bf16),
            pltpu.VMEM((3, 4 * ROWS, COLS), bf16),
            pltpu.VMEM((4 * ROWS, COLS), bf16),
            pltpu.VMEM((4, 8, TOK), jnp.float32),
            *sems,
        ],
        compiler_params=pltpu.CompilerParams(
            collective_id=0, has_side_effects=True, vmem_limit_bytes=52 * 2**20
        ),
        cost_estimate=pl.CostEstimate(
            flops=4 * TOK * DW * FW, bytes_accessed=10 * 2**20, transcendentals=TOK * FW
        ),
    )(inputs, token_ids, upstream, weight)


def outer_update(frag_index, global_params, local_params, momentum):
    fragment = frag_index[0]
    chosen = lax.dynamic_index_in_dim(global_params, fragment, 0, keepdims=False)
    local_now = lax.dynamic_index_in_dim(local_params[0], fragment, 0, keepdims=False)
    moment_now = lax.dynamic_index_in_dim(momentum, fragment, 0, keepdims=False)
    replicas = lax.axis_size("replica")
    difference = chosen - local_now
    delta = lax.psum(difference.astype(jnp.bfloat16), "replica").astype(jnp.float32) / replicas
    new_momentum = 0.9 * moment_now + delta
    new_global = chosen - 0.7 * (delta + 0.9 * new_momentum)
    return (new_global, new_momentum)


def local(inputs, token_ids, upstream, weight, frag_index, global_params, local_params, momentum):
    weight_grad = inner_grad(inputs, token_ids, upstream, weight)
    new_global, new_momentum = outer_update(frag_index, global_params, local_params, momentum)
    return (weight_grad, new_global, new_momentum)


def solution(mesh):
    placed = (
        P("replica", "fsdp", None),
        P("replica", "fsdp"),
        P("replica", "fsdp", None),
        P("replica", "fsdp", None),
        P(),
        P(None, "fsdp"),
        P("replica", None, "fsdp"),
        P(None, "fsdp"),
    )
    return jax.shard_map(
        local,
        mesh=mesh,
        in_specs=placed,
        out_specs=(P("replica", "fsdp", None), P("fsdp"), P("fsdp")),
        check_vma=False,
    )
```

```python
import functools

import jax
import jax.numpy as jnp
from jax import lax
from jax.experimental import pallas as pl
from jax.experimental.pallas import tpu as pltpu
from jax.sharding import PartitionSpec as P

MESH = pl.DeviceIdType.MESH
TOK, DW, FW = 512, 1536, 6144
ROWS = 48
HALF = 768
COLS = 1536
WIDE = 256
CHUNKS = tuple((c, WIDE) for c in range(0, COLS, WIDE))
FIRST = ((0, WIDE), (WIDE, COLS - WIDE))
W_OVER_FIRST = (5,)
G_OVER_LAST = (4, 5)
DIST = (1, 3, 2)
MB = 256


def kernel(
    x_hbm, ids_hbm, up_hbm, w_hbm, frag_ref, gp_hbm, lp_hbm, mo_hbm,
    out_hbm, new_global, new_momentum,
    X, XT, U, W, E, G, RY, RX, T, T2, WY, K, IDS,
    GP, LP, MO, CHOSEN, MOMENT, DIFF, DPAIR, PAIR, OTHER, DELTA,
    NEW_G, NEW_M, plan_sem, o_s, o_r, own_sem, a_s, a_r, k_s, k_r, x_s, x_r, u_s, u_r,
    b_s, b_r, c_s, c_r, d_s, d_r, e_s, e_r, f_s, f_r,
    v_s, v_r, g_s, g_r,
):
    ids_in = pltpu.make_async_copy(ids_hbm, IDS, plan_sem.at[3])
    ids_in.start()
    replica = lax.axis_index("replica")
    core, low = lax.rem(replica, 2), lax.div(replica, 2)
    me = lax.axis_index("fsdp")
    h, z, x = lax.div(me, 16), lax.rem(lax.div(me, 4), 4), lax.rem(me, 4)
    p = z + core * (x - z)
    q = x + core * (z - x)

    def place(hh, pp, qq):
        return hh * 16 + (pp + core * (qq - pp)) * 4 + (qq + core * (pp - qq))

    def rows(hh, pp, qq):
        return pl.ds(pl.multiple_of(place(hh, pp, qq) * ROWS, 16), ROWS)

    def ahead(a, d):
        return lax.rem(a + d, 4)

    def remote(src, dst, send, recv, device, axis="fsdp"):
        return pltpu.make_async_remote_copy(
            src_ref=src, dst_ref=dst, send_sem=send, recv_sem=recv,
            device_id={axis: device}, device_id_type=MESH,
        )

    sent = []

    def quarter(pp, c0, cw):
        return pl.ds(pl.multiple_of(pp * COLS + c0, 128), cw)

    barrier = pltpu.get_barrier_semaphore()
    near = [place(h, ahead(p, d), q) for d in DIST]
    side = [place(h, p, ahead(q, d)) for d in DIST]
    over = place(1 - h, p, q)
    for device in near + side + [over]:
        pl.semaphore_signal(barrier, inc=1, device_id={"fsdp": device}, device_id_type=MESH)
    twin, mate = low * 2 + 1 - core, (1 - low) * 2 + core
    for device in (twin, mate):
        pl.semaphore_signal(barrier, inc=1, device_id={"replica": device}, device_id_type=MESH)
    pl.semaphore_wait(barrier, 9)

    own = []
    weight_in = []
    for n, (c0, cw) in enumerate(FIRST):
        place_w = W.at[rows(h, p, q), pl.ds(c0, cw)]
        copies = []
        for i, d in enumerate(DIST):
            copy = remote(
                w_hbm.at[0, :, quarter(ahead(p, d), c0, cw)], place_w,
                a_s.at[n, i], a_r.at[n, i], near[i],
            )
            copy.start()
            copies.append(copy)
        mine = pltpu.make_async_copy(w_hbm.at[0, :, quarter(p, c0, cw)], place_w, own_sem.at[n])
        mine.start()
        weight_in.append((mine, copies))
        sent += copies

    cross_in = {}
    for n in W_OVER_FIRST:
        c0, cw = CHUNKS[n]
        cols = pl.ds(c0, cw)
        for pp in range(4):
            remote(w_hbm.at[0, :, quarter(pp, c0, cw)], WY.at[pp, :, cols], v_s.at[n], v_r.at[n], over).start()
        cross_in[n] = remote(WY.at[:, :, cols], WY.at[:, :, cols], v_s.at[n], v_r.at[n], over)
        sent.append(cross_in[n])

    ids_in.wait()
    K[p] = jnp.broadcast_to((IDS[...] != 0).astype(jnp.float32), (8, TOK))
    x_in, k_in, u_in = [], [], []
    for i in range(2):
        x_in.append(remote(x_hbm.at[0], X.at[p], x_s.at[i], x_r.at[i], near[i]))
        x_in[i].start()
    x_own = pltpu.make_async_copy(x_hbm.at[0], X.at[p], own_sem.at[2])
    x_own.start()
    for i in range(3):
        k_in.append(remote(K.at[p], K.at[p], k_s.at[i], k_r.at[i], near[i]))
        k_in[i].start()

    def send_up(n):
        c0, cw = CHUNKS[n]
        there = U.at[p, :, pl.ds(c0, cw)]
        copies = []
        for i, d in enumerate(DIST):
            copy = remote(
                up_hbm.at[0, :, quarter(ahead(p, d), c0, cw)], there,
                u_s.at[n, i], u_r.at[n, i], near[i],
            )
            copy.start()
            copies.append(copy)
        u_in.append(copies)
        sent.extend(copies)

    send_up(0)
    u_own = pltpu.make_async_copy(up_hbm.at[0, :, quarter(p, 0, COLS)], U.at[p], own_sem.at[3])
    u_own.start()
    blocks = [p] + [lax.rem(p - d + 4, 4) for d in DIST]

    def pass_on():
        for i in range(2):
            x_in[i].wait_recv()
            part = X.at[blocks[i + 1], pl.ds(256 * i, 256)]
            x_in.append(remote(part, part, x_s.at[2 + i], x_r.at[2 + i], near[i]))
            x_in[2 + i].start()
            sent.append(x_in[2 + i])

    sent += x_in + k_in
    plan_in = []
    for i, (source, target) in enumerate(((gp_hbm, GP), (lp_hbm.at[0], LP), (mo_hbm, MO))):
        plan_in.append(pltpu.make_async_copy(source, target, plan_sem.at[i]))
        plan_in[i].start()

    mine_half = pl.ds(pl.multiple_of(core * 256, 16), 256)
    twin_half = pl.ds(pl.multiple_of((1 - core) * 256, 16), 256)
    pair_in = remote(DIFF.at[twin_half], DPAIR, o_s.at[0], o_r.at[0], twin, "replica")
    other_in = remote(PAIR, OTHER, o_s.at[1], o_r.at[1], mate, "replica")
    delta_in = remote(DELTA.at[mine_half], DELTA.at[mine_half], o_s.at[2], o_r.at[2], twin, "replica")
    sent += [pair_in, other_in, delta_in]

    def plan_pick():
        for copy in plan_in:
            copy.wait()
        fragment = frag_ref[0]

        def step(j, carry):
            cols = pl.ds(pl.multiple_of(j * 2048, 2048), 2048)
            part = pl.ds(pl.multiple_of(j * 16, 16), 16)
            chosen = GP[pl.ds(fragment, 1), cols].reshape(16, 128)
            CHOSEN[part, :] = chosen
            MOMENT[part, :] = MO[pl.ds(fragment, 1), cols].reshape(16, 128)
            DIFF[part, :] = (chosen - LP[pl.ds(fragment, 1), cols].reshape(16, 128)).astype(jnp.bfloat16)
            return carry

        lax.fori_loop(0, 32, step, 0)
        pair_in.start()

    def plan_pair():
        pair_in.wait_recv()
        PAIR[...] = (DIFF[mine_half, :].astype(jnp.float32) + DPAIR[...].astype(jnp.float32)).astype(jnp.bfloat16)
        other_in.start()

    def plan_sum():
        other_in.wait_recv()
        total = PAIR[...].astype(jnp.float32) + OTHER[...].astype(jnp.float32)
        DELTA[mine_half, :] = total * 0.25
        delta_in.start()

    def plan_update():
        delta_in.wait_recv()
        delta = DELTA[...]
        moment = 0.9 * MOMENT[...] + delta
        NEW_M[...] = moment
        NEW_G[...] = CHOSEN[...] - 0.7 * (delta + 0.9 * moment)
        for i, (source, target) in enumerate(((NEW_G, new_global), (NEW_M, new_momentum))):
            copy = pltpu.make_async_copy(source, target, plan_sem.at[i])
            copy.start()
            own.append(copy)

    def arrive(copies):
        for copy in copies:
            copy.wait_recv()

    side_in = []

    def planes(n):
        return range(2) if n in W_OVER_FIRST else [h]

    def to_side(n):
        c0, cw = CHUNKS[n]
        cols = pl.ds(c0, cw)
        totals = []
        for i in range(3):
            for hh in planes(n):
                for pp in range(4):
                    part = W.at[rows(hh, pp, q), cols]
                    remote(part, part, b_s.at[n, i], b_r.at[n, i], side[i]).start()
            whole = W.at[pl.ds(0, 4 * ROWS * len(planes(n))), cols]
            totals.append(remote(whole, whole, b_s.at[n, i], b_r.at[n, i], side[i]))
        side_in.append(totals)
        sent.extend(totals)

    over_in = {}

    def to_over(n):
        arrive(side_in[n])
        c0, cw = CHUNKS[n]
        half = W.at[pl.ds(pl.multiple_of(h * HALF, 16), HALF), pl.ds(c0, cw)]
        copy = remote(half, half, c_s.at[n], c_r.at[n], over)
        copy.start()
        over_in[n] = [copy]
        sent.append(copy)

    again_in = {}

    def to_near_again(n):
        cross_in[n].wait_recv()
        c0, cw = CHUNKS[n]
        cols = pl.ds(c0, cw)
        there = W.at[rows(1 - h, p, q), cols]
        copies = []
        for i, d in enumerate(DIST):
            copies.append(remote(WY.at[ahead(p, d), :, cols], there, g_s.at[n, i], g_r.at[n, i], near[i]))
            copies[i].start()
        mine = pltpu.make_async_copy(WY.at[p, :, cols], there, own_sem.at[4 + len(CHUNKS) + n])
        mine.start()
        again_in[n] = (mine, copies)
        sent.extend(copies)

    def to_side_again(n):
        again_in[n][0].wait()
        arrive(again_in[n][1])
        to_side(n)
        over_in[n] = side_in[n]

    def turn(t):
        kept = K[t][0:1, :].astype(jnp.bfloat16)

        def step(j, carry):
            cols = pl.ds(pl.multiple_of(j * 256, 256), 256)
            XT[t, cols, :] = jnp.transpose(X[t, :, cols]) * kept
            return carry

        lax.fori_loop(0, DW // 256, step, 0)

    weight_in[0][0].wait()
    arrive(weight_in[0][1])
    to_side(0)
    weight_in[1][0].wait()
    arrive(weight_in[1][1])
    plain = [n for n in range(len(CHUNKS)) if n not in W_OVER_FIRST]
    for n in plain[1:]:
        to_side(n)
    for n in W_OVER_FIRST:
        to_near_again(n)
    plan_pick()
    to_over(0)
    x_own.wait()
    turn(p)
    to_over(1)
    plan_pair()
    to_over(2)
    pass_on()
    for n in range(1, len(CHUNKS)):
        send_up(n)
    for n in plain[3:]:
        to_over(n)
    for n in W_OVER_FIRST:
        to_side_again(n)
    plan_sum()
    u_own.wait()
    k_in[0].wait_recv()
    turn(blocks[1])
    k_in[1].wait_recv()
    turn(blocks[2])
    k_in[2].wait_recv()
    x_in[2].wait_recv()
    x_in[3].wait_recv()
    turn(blocks[3])
    plan_update()

    def forward(n, t):
        c0, cw = CHUNKS[n]

        def step(m, carry):
            part = pl.ds(pl.multiple_of(m * MB, MB), MB)
            pre = jnp.dot(X[t, part, :], W[:, c0 : c0 + cw], preferred_element_type=jnp.float32)
            sig = jax.nn.sigmoid(pre)
            deriv = sig * (1.0 + pre * (1.0 - sig))
            eff = U[t, part, c0 : c0 + cw].astype(jnp.float32) * deriv
            E[t, part, 0:cw] = eff.astype(jnp.bfloat16)
            return carry

        lax.fori_loop(0, TOK // MB, step, 0)

    def grad(n, half):
        c0, cw = CHUNKS[n]

        def step(m, carry):
            part = pl.ds(pl.multiple_of(half * HALF + m * 256, 256), 256)
            acc = jnp.dot(XT[0, part, :], E[0, :, 0:cw], preferred_element_type=jnp.float32)
            for t in range(1, 4):
                acc += jnp.dot(XT[t, part, :], E[t, :, 0:cw], preferred_element_type=jnp.float32)
            G[part, c0 : c0 + cw] = acc.astype(jnp.bfloat16)
            return carry

        lax.fori_loop(0, HALF // 256, step, 0)

    back_in = {}

    def compute(n):
        c0, cw = CHUNKS[n]
        arrive(over_in[n])
        forward(n, blocks[0])
        for i in range(3):
            u_in[n][i].wait_recv()
            forward(n, blocks[i + 1])
        grad(n, 1 - h)
        if n in G_OVER_LAST:
            grad(n, h)
            add_side(n, range(2))
            return
        copy = remote(
            G.at[pl.ds(pl.multiple_of((1 - h) * HALF, 16), HALF), pl.ds(c0, cw)],
            RY.at[:, pl.ds(c0, cw)], d_s.at[n], d_r.at[n], over,
        )
        copy.start()
        back_in[n] = copy
        sent.append(copy)
        grad(n, h)

    sums_in = {}

    def add_side(n, both):
        c0, cw = CHUNKS[n]
        cols = pl.ds(c0, cw)
        totals = []
        for i, d in enumerate(DIST):
            for j, hh in enumerate(both):
                for pp in range(4):
                    remote(
                        G.at[rows(hh, pp, ahead(q, d)), cols],
                        RX.at[i, pl.ds((4 * j + pp) * ROWS, ROWS), cols],
                        e_s.at[n, i], e_r.at[n, i], side[i],
                    ).start()
            whole = RX.at[i, pl.ds(0, 4 * ROWS * len(both)), cols]
            totals.append(remote(whole, whole, e_s.at[n, i], e_r.at[n, i], side[i]))
        sums_in[n] = totals
        sent.extend(totals)

    def reduce_over(n):
        c0, cw = CHUNKS[n]
        back_in[n].wait_recv()

        def step(m, carry):
            here = pl.ds(pl.multiple_of(h * HALF + m * 64, 64), 64)
            there = pl.ds(pl.multiple_of(m * 64, 64), 64)
            total = G[here, c0 : c0 + cw].astype(jnp.float32) + RY[there, c0 : c0 + cw].astype(jnp.float32)
            G[here, c0 : c0 + cw] = total.astype(jnp.bfloat16)
            return carry

        lax.fori_loop(0, HALF // 64, step, 0)
        add_side(n, [h])

    def side_sum(n, hh, first, target):
        c0, cw = CHUNKS[n]

        def step(pp, carry):
            part = pl.ds(pl.multiple_of(first + pp * ROWS, 16), ROWS)
            total = G[rows(hh, pp, q), c0 : c0 + cw].astype(jnp.float32)
            for i in range(3):
                total += RX[i, part, c0 : c0 + cw].astype(jnp.float32)
            target[pl.ds(pl.multiple_of(pp * ROWS, 16), ROWS), c0 : c0 + cw] = total.astype(jnp.bfloat16)
            return carry

        lax.fori_loop(0, 4, step, 0)

    last_in = []

    def finish(n):
        c0, cw = CHUNKS[n]
        there = out_hbm.at[0, :, quarter(p, c0, cw)]
        copies = []
        for i, d in enumerate(DIST):
            part = pl.ds(pl.multiple_of(ahead(p, d) * ROWS, 16), ROWS)
            copy = remote(T.at[part, pl.ds(c0, cw)], there, f_s.at[n, i], f_r.at[n, i], near[i])
            copy.start()
            copies.append(copy)
        part = pl.ds(pl.multiple_of(p * ROWS, 16), ROWS)
        mine = pltpu.make_async_copy(T.at[part, pl.ds(c0, cw)], there, own_sem.at[4 + n])
        mine.start()
        own.append(mine)
        last_in.append(copies)
        sent.extend(copies)

    def reduce_side(n):
        arrive(sums_in[n])
        if n not in G_OVER_LAST:
            side_sum(n, h, 0, T)
            finish(n)
            return
        c0, cw = CHUNKS[n]
        side_sum(n, 1 - h, (1 - h) * 4 * ROWS, T2)
        cols = pl.ds(c0, cw)
        copy = remote(T2.at[:, cols], RY.at[pl.ds(0, 4 * ROWS), cols], d_s.at[n], d_r.at[n], over)
        copy.start()
        back_in[n] = copy
        sent.append(copy)
        side_sum(n, h, h * 4 * ROWS, T)

    def reduce_last(n):
        c0, cw = CHUNKS[n]
        back_in[n].wait_recv()

        def step(pp, carry):
            part = pl.ds(pl.multiple_of(pp * ROWS, 16), ROWS)
            total = T[part, c0 : c0 + cw].astype(jnp.float32) + RY[part, c0 : c0 + cw].astype(jnp.float32)
            T[part, c0 : c0 + cw] = total.astype(jnp.bfloat16)
            return carry

        lax.fori_loop(0, 4, step, 0)
        finish(n)

    compute(0)
    compute(1)
    compute(2)
    reduce_over(0)
    compute(3)
    reduce_over(1)
    reduce_side(0)
    compute(4)
    reduce_over(2)
    reduce_side(1)
    compute(5)
    reduce_side(4)
    reduce_over(3)
    reduce_side(2)
    reduce_side(5)
    reduce_last(4)
    reduce_side(3)
    reduce_last(5)
    for copies in last_in:
        arrive(copies)
    for mine in own:
        mine.wait()
    for copy in sent:
        copy.wait_send()


def local(inputs, token_ids, upstream, weight, frag_index, global_params, local_params, momentum):
    n = len(CHUNKS)
    bf16, f32 = jnp.bfloat16, jnp.float32
    sems = [pltpu.SemaphoreType.DMA((4,))]
    sems += [pltpu.SemaphoreType.DMA((3,))] * 2
    sems += [pltpu.SemaphoreType.DMA((4 + 2 * n,))]
    for shape in ((2, 3), (3,), (4,), (n, 3), (n, 3), (n,), (n,), (n, 3), (n, 3), (n,), (n, 3)):
        sems += [pltpu.SemaphoreType.DMA(shape)] * 2
    hbm = pl.BlockSpec(memory_space=pltpu.HBM)
    span = global_params.shape[1]
    weight_grad, new_global, new_momentum = pl.pallas_call(
        kernel,
        name="inner_grad_outer_update",
        out_shape=(
            jax.ShapeDtypeStruct((1, ROWS, FW), bf16),
            jax.ShapeDtypeStruct((512, 128), f32),
            jax.ShapeDtypeStruct((512, 128), f32),
        ),
        in_specs=[hbm, hbm, hbm, hbm, pl.BlockSpec(memory_space=pltpu.SMEM), hbm, hbm, hbm],
        out_specs=[pl.BlockSpec(memory_space=pl.ANY)] * 3,
        scratch_shapes=[
            pltpu.VMEM((4, TOK, DW), bf16),
            pltpu.VMEM((4, DW, TOK), bf16),
            pltpu.VMEM((4, TOK, COLS), bf16),
            pltpu.VMEM((DW, COLS), bf16),
            pltpu.VMEM((4, TOK, WIDE), bf16),
            pltpu.VMEM((DW, COLS), bf16),
            pltpu.VMEM((HALF, COLS), bf16),
            pltpu.VMEM((3, 8 * ROWS, COLS), bf16),
            pltpu.VMEM((4 * ROWS, COLS), bf16),
            pltpu.VMEM((4 * ROWS, COLS), bf16),
            pltpu.VMEM((4, ROWS, COLS), bf16),
            pltpu.VMEM((4, 8, TOK), f32),
            pltpu.VMEM((1, TOK), jnp.int32),
            pltpu.VMEM((16, span), f32),
            pltpu.VMEM((16, span), f32),
            pltpu.VMEM((16, span), f32),
            pltpu.VMEM((512, 128), f32),
            pltpu.VMEM((512, 128), f32),
            pltpu.VMEM((512, 128), bf16),
            pltpu.VMEM((256, 128), bf16),
            pltpu.VMEM((256, 128), bf16),
            pltpu.VMEM((256, 128), bf16),
            pltpu.VMEM((512, 128), f32),
            pltpu.VMEM((512, 128), f32),
            pltpu.VMEM((512, 128), f32),
            *sems,
        ],
        compiler_params=pltpu.CompilerParams(
            collective_id=0, has_side_effects=True, vmem_limit_bytes=51 * 2**20
        ),
        cost_estimate=pl.CostEstimate(
            flops=4 * TOK * DW * FW, bytes_accessed=22 * 2**20, transcendentals=TOK * FW
        ),
    )(inputs, token_ids, upstream, weight, frag_index, global_params, local_params, momentum)
    return (weight_grad, new_global.reshape(span), new_momentum.reshape(span))


def solution(mesh):
    placed = (
        P("replica", "fsdp", None),
        P("replica", "fsdp"),
        P("replica", "fsdp", None),
        P("replica", "fsdp", None),
        P(),
        P(None, "fsdp"),
        P("replica", None, "fsdp"),
        P(None, "fsdp"),
    )
    return jax.shard_map(
        local,
        mesh=mesh,
        in_specs=placed,
        out_specs=(P("replica", "fsdp", None), P("fsdp"), P("fsdp")),
        check_vma=False,
    )
```

```python
import functools

import jax
import jax.numpy as jnp
from jax import lax
from jax.experimental import pallas as pl
from jax.experimental.pallas import tpu as pltpu
from jax.sharding import PartitionSpec as P

MESH = pl.DeviceIdType.MESH
TOK, DW, FW = 512, 1536, 6144
ROWS = 48
HALF = 768
COLS = 1536
WIDE = 256
CHUNKS = tuple((c, WIDE) for c in range(0, COLS, WIDE))
FIRST = ((0, WIDE), (WIDE, COLS - WIDE))
W_OVER_FIRST = (5,)
G_OVER_LAST = (4, 5)
DIST = (1, 3, 2)
B_DIRECT = (0,)
EARLY = (
    ("send_up", 0), ("weight_ready", 0), ("to_side", 0), ("weight_ready", 1), ("to_side", 1), ("to_side", 2),
    ("to_near_again", 5), ("pick",), ("pass_side", 1), ("to_over", 0), ("to_side", 3), ("pass_side", 2),
    ("to_over", 1), ("to_side", 4), ("turn_own",), ("pass_side", 3), ("to_over", 2), ("pair",), ("pass_side", 4),
    ("pass_on", 0), ("pass_on", 1), ("send_up", 1), ("pass_up", 0), ("send_up", 2), ("to_over", 3),
    ("to_side_again", 5), ("to_over", 4), ("sum",), ("up_own",), ("turn_near", 0), ("turn_near", 1),
    ("pass_up", 1), ("send_up", 3), ("pass_side_again", 5), ("update",), ("turn_far",),
)
LATE = (
    ("compute", 0), ("pass_up", 2), ("send_up", 4), ("compute", 1), ("pass_up", 3), ("send_up", 5), ("compute", 2),
    ("pass_up", 4), ("over", 0), ("compute", 3), ("pass_up", 5), ("over", 1), ("side", 0), ("compute", 4),
    ("compute", 5), ("over", 2), ("far_plane", 4), ("side", 1), ("drain",), ("far_plane", 5), ("own_plane", 4), ("over", 3),
    ("side", 2), ("own_plane", 5), ("last", 4), ("last", 5), ("side", 3),
)
MB = 512
GM = 384


def kernel(
    x_hbm, ids_hbm, up_hbm, w_hbm, frag_ref, gp_hbm, lp_hbm, mo_hbm,
    out_hbm, new_global, new_momentum,
    X, XT, U, W, E, G, RY, RX, T, T2, WY, UR, K, IDS,
    GP, LP, MO, CHOSEN, MOMENT, DIFF, DPAIR, PAIR, OTHER, DELTA,
    NEW_G, NEW_M, plan_sem, o_s, o_r, own_sem, a_s, a_r, k_s, k_r, x_s, x_r, u_s, u_r,
    b_s, b_r, c_s, c_r, d_s, d_r, e_s, e_r, f_s, f_r,
    v_s, v_r, g_s, g_r, r_s, r_r,
):
    ids_in = pltpu.make_async_copy(ids_hbm, IDS, plan_sem.at[3])
    ids_in.start()
    replica = lax.axis_index("replica")
    core, low = lax.rem(replica, 2), lax.div(replica, 2)
    me = lax.axis_index("fsdp")
    h, z, x = lax.div(me, 16), lax.rem(lax.div(me, 4), 4), lax.rem(me, 4)
    p = z + core * (x - z)
    q = x + core * (z - x)

    def place(hh, pp, qq):
        return hh * 16 + (pp + core * (qq - pp)) * 4 + (qq + core * (pp - qq))

    def rows(hh, pp, qq):
        return pl.ds(pl.multiple_of(place(hh, pp, qq) * ROWS, 16), ROWS)

    def ahead(a, d):
        return lax.rem(a + d, 4)

    def remote(src, dst, send, recv, device, axis="fsdp"):
        return pltpu.make_async_remote_copy(
            src_ref=src, dst_ref=dst, send_sem=send, recv_sem=recv,
            device_id={axis: device}, device_id_type=MESH,
        )

    own, sent = [], []

    def drain():
        for mine in own:
            mine.wait()
        for copy in sent:
            copy.wait_send()
        own.clear()
        sent.clear()

    def quarter(pp, c0, cw):
        return pl.ds(pl.multiple_of(pp * COLS + c0, 128), cw)

    barrier = pltpu.get_barrier_semaphore()
    near = [place(h, ahead(p, d), q) for d in DIST]
    side = [place(h, p, ahead(q, d)) for d in DIST]
    over = place(1 - h, p, q)
    for device in near + side + [over]:
        pl.semaphore_signal(barrier, inc=1, device_id={"fsdp": device}, device_id_type=MESH)
    twin, mate = low * 2 + 1 - core, (1 - low) * 2 + core
    for device in (twin, mate):
        pl.semaphore_signal(barrier, inc=1, device_id={"replica": device}, device_id_type=MESH)
    pl.semaphore_wait(barrier, 9)

    weight_in = []
    for n, (c0, cw) in enumerate(FIRST):
        place_w = W.at[rows(h, p, q), pl.ds(c0, cw)]
        copies = []
        for i, d in enumerate(DIST):
            copy = remote(
                w_hbm.at[0, :, quarter(ahead(p, d), c0, cw)], place_w,
                a_s.at[n, i], a_r.at[n, i], near[i],
            )
            copy.start()
            copies.append(copy)
        mine = pltpu.make_async_copy(w_hbm.at[0, :, quarter(p, c0, cw)], place_w, own_sem.at[n])
        mine.start()
        weight_in.append((mine, copies))
        sent += copies

    cross_in = {}
    for n in W_OVER_FIRST:
        c0, cw = CHUNKS[n]
        cols = pl.ds(c0, cw)
        for pp in range(4):
            remote(w_hbm.at[0, :, quarter(pp, c0, cw)], WY.at[pp, :, cols], v_s.at[n], v_r.at[n], over).start()
        cross_in[n] = remote(WY.at[:, :, cols], WY.at[:, :, cols], v_s.at[n], v_r.at[n], over)
        sent.append(cross_in[n])

    ids_in.wait()
    K[p] = jnp.broadcast_to((IDS[...] != 0).astype(jnp.float32), (8, TOK))
    x_in, k_in, u_in = [], [], {}
    for i in range(2):
        x_in.append(remote(x_hbm.at[0], X.at[p], x_s.at[i], x_r.at[i], near[i]))
        x_in[i].start()
    x_own = pltpu.make_async_copy(x_hbm.at[0], X.at[p], own_sem.at[2])
    x_own.start()
    for i in range(3):
        k_in.append(remote(K.at[p], K.at[p], k_s.at[i], k_r.at[i], near[i]))
        k_in[i].start()

    relay_in = {}

    def send_up(n):
        c0, cw = CHUNKS[n]
        there = U.at[p, :, pl.ds(c0, cw)]
        u_in[n], relay_in[n] = [], []
        far = quarter(ahead(p, 2), c0, cw)
        for i in range(2):
            copy = remote(
                up_hbm.at[0, :, quarter(ahead(p, DIST[i]), c0, cw)], there,
                u_s.at[n, i], u_r.at[n, i], near[i],
            )
            half = remote(up_hbm.at[0, pl.ds(256 * i, 256), far], UR.at[i, n], r_s.at[n, i], r_r.at[n, i], near[i])
            copy.start()
            half.start()
            u_in[n].append(copy)
            relay_in[n].append(half)
        sent.extend(u_in[n] + relay_in[n])

    def pass_up(n):
        c0, cw = CHUNKS[n]
        for i in range(2):
            relay_in[n][i].wait_recv()
            there = U.at[blocks[i + 1], pl.ds(256 * i, 256), pl.ds(c0, cw)]
            copy = remote(UR.at[i, n], there, u_s.at[n, 2 + i], u_r.at[n, 2 + i], near[i])
            copy.start()
            u_in[n].append(copy)
            sent.append(copy)

    u_own = pltpu.make_async_copy(up_hbm.at[0, :, quarter(p, 0, COLS)], U.at[p], own_sem.at[3])
    u_own.start()
    blocks = [p] + [lax.rem(p - d + 4, 4) for d in DIST]

    def pass_on(i):
        x_in[i].wait_recv()
        part = X.at[blocks[i + 1], pl.ds(256 * i, 256)]
        x_in.append(remote(part, part, x_s.at[2 + i], x_r.at[2 + i], near[i]))
        x_in[2 + i].start()
        sent.append(x_in[2 + i])

    sent += x_in + k_in
    plan_in = []
    for i, (source, target) in enumerate(((gp_hbm, GP), (lp_hbm.at[0], LP), (mo_hbm, MO))):
        plan_in.append(pltpu.make_async_copy(source, target, plan_sem.at[i]))
        plan_in[i].start()

    mine_half = pl.ds(pl.multiple_of(core * 256, 16), 256)
    twin_half = pl.ds(pl.multiple_of((1 - core) * 256, 16), 256)
    pair_in = remote(DIFF.at[twin_half], DPAIR, o_s.at[0], o_r.at[0], twin, "replica")
    other_in = remote(PAIR, OTHER, o_s.at[1], o_r.at[1], mate, "replica")
    delta_in = remote(DELTA.at[mine_half], DELTA.at[mine_half], o_s.at[2], o_r.at[2], twin, "replica")
    sent += [pair_in, other_in, delta_in]

    def plan_pick():
        for copy in plan_in:
            copy.wait()
        fragment = frag_ref[0]

        def step(j, carry):
            cols = pl.ds(pl.multiple_of(j * 2048, 2048), 2048)
            part = pl.ds(pl.multiple_of(j * 16, 16), 16)
            chosen = GP[pl.ds(fragment, 1), cols].reshape(16, 128)
            CHOSEN[part, :] = chosen
            MOMENT[part, :] = MO[pl.ds(fragment, 1), cols].reshape(16, 128)
            DIFF[part, :] = (chosen - LP[pl.ds(fragment, 1), cols].reshape(16, 128)).astype(jnp.bfloat16)
            return carry

        lax.fori_loop(0, 32, step, 0)
        pair_in.start()

    def plan_pair():
        pair_in.wait_recv()
        PAIR[...] = (DIFF[mine_half, :].astype(jnp.float32) + DPAIR[...].astype(jnp.float32)).astype(jnp.bfloat16)
        other_in.start()

    def plan_sum():
        other_in.wait_recv()
        total = PAIR[...].astype(jnp.float32) + OTHER[...].astype(jnp.float32)
        DELTA[mine_half, :] = total * 0.25
        delta_in.start()

    def plan_update():
        delta_in.wait_recv()
        delta = DELTA[...]
        moment = 0.9 * MOMENT[...] + delta
        NEW_M[...] = moment
        NEW_G[...] = CHOSEN[...] - 0.7 * (delta + 0.9 * moment)
        for i, (source, target) in enumerate(((NEW_G, new_global), (NEW_M, new_momentum))):
            copy = pltpu.make_async_copy(source, target, plan_sem.at[i])
            copy.start()
            own.append(copy)

    def arrive(copies):
        for copy in copies:
            copy.wait_recv()

    side_in = {}

    def planes(n):
        return range(2) if n in W_OVER_FIRST else [h]

    def to_side(n):
        c0, cw = CHUNKS[n]
        cols = pl.ds(c0, cw)
        totals = []
        for i in range(3 if n in B_DIRECT else 2):
            for hh in planes(n):
                for pp in range(4):
                    part = W.at[rows(hh, pp, q), cols]
                    remote(part, part, b_s.at[n, i], b_r.at[n, i], side[i]).start()
            whole = W.at[pl.ds(0, 4 * ROWS * len(planes(n))), cols]
            totals.append(remote(whole, whole, b_s.at[n, i], b_r.at[n, i], side[i]))
        side_in[n] = totals
        sent.extend(totals)

    def pass_side(n):
        c0, cw = CHUNKS[n]
        cols = pl.ds(c0, cw)
        for i in range(2):
            side_in[n][i].wait_recv()
            for hh in planes(n):
                for pp in (2 * i, 2 * i + 1):
                    part = W.at[rows(hh, pp, lax.rem(q - DIST[i] + 4, 4)), cols]
                    remote(part, part, b_s.at[n, 2 + i], b_r.at[n, 2 + i], side[i]).start()
            whole = W.at[pl.ds(0, 2 * ROWS * len(planes(n))), cols]
            total = remote(whole, whole, b_s.at[n, 2 + i], b_r.at[n, 2 + i], side[i])
            side_in[n].append(total)
            sent.append(total)

    over_in = {}

    def to_over(n):
        arrive(side_in[n] if n in B_DIRECT else side_in[n][2:])
        c0, cw = CHUNKS[n]
        half = W.at[pl.ds(pl.multiple_of(h * HALF, 16), HALF), pl.ds(c0, cw)]
        copy = remote(half, half, c_s.at[n], c_r.at[n], over)
        copy.start()
        over_in[n] = [copy]
        sent.append(copy)

    again_in = {}

    def to_near_again(n):
        cross_in[n].wait_recv()
        c0, cw = CHUNKS[n]
        cols = pl.ds(c0, cw)
        there = W.at[rows(1 - h, p, q), cols]
        copies = []
        for i, d in enumerate(DIST):
            copies.append(remote(WY.at[ahead(p, d), :, cols], there, g_s.at[n, i], g_r.at[n, i], near[i]))
            copies[i].start()
        mine = pltpu.make_async_copy(WY.at[p, :, cols], there, own_sem.at[4 + len(CHUNKS) + n])
        mine.start()
        again_in[n] = (mine, copies)
        sent.extend(copies)

    def to_side_again(n):
        again_in[n][0].wait()
        arrive(again_in[n][1])
        to_side(n)

    def pass_side_again(n):
        pass_side(n)
        over_in[n] = side_in[n][2:]

    def turn(t):
        kept = K[t][0:1, :].astype(jnp.bfloat16)

        def step(j, carry):
            cols = pl.ds(pl.multiple_of(j * 256, 256), 256)
            XT[cols, pl.ds(pl.multiple_of(t * TOK, TOK), TOK)] = jnp.transpose(X[t, :, cols]) * kept
            return carry

        lax.fori_loop(0, DW // 256, step, 0)

    def weight_ready(n):
        weight_in[n][0].wait()
        arrive(weight_in[n][1])

    def turn_own():
        x_own.wait()
        turn(p)

    def turn_near(i):
        k_in[i].wait_recv()
        turn(blocks[i + 1])

    def turn_far():
        k_in[2].wait_recv()
        x_in[2].wait_recv()
        x_in[3].wait_recv()
        turn(blocks[3])

    early = {
        "weight_ready": weight_ready, "to_side": to_side, "to_near_again": to_near_again, "to_over": to_over,
        "to_side_again": to_side_again, "send_up": send_up, "pass_on": pass_on, "pass_up": pass_up, "pass_side": pass_side, "pass_side_again": pass_side_again, "turn_own": turn_own,
        "turn_near": turn_near, "turn_far": turn_far, "pick": plan_pick, "pair": plan_pair, "sum": plan_sum,
        "update": plan_update, "up_own": u_own.wait,
    }
    for name, *which in EARLY:
        early[name](*which)

    def forward(n):
        c0, cw = CHUNKS[n]
        steps = TOK // MB

        def step(k, carry):
            b, m = lax.div(k, steps), lax.rem(k, steps)
            for i in range(2):
                pl.when(k == (i + 1) * steps)(u_in[n][i].wait_recv)
            pl.when(k == 3 * steps)(lambda: arrive(u_in[n][2:]))
            t = lax.rem(p - (b + lax.div(b, 2) - 2 * lax.div(b, 3)) + 4, 4)
            part = pl.ds(pl.multiple_of(m * MB, MB), MB)
            pre = jnp.dot(X[t, part, :], W[:, c0 : c0 + cw], preferred_element_type=jnp.float32)
            sig = 0.5 + 0.5 * jnp.tanh(0.5 * pre)
            deriv = sig * (1.0 + pre * (1.0 - sig))
            eff = U[t, part, c0 : c0 + cw].astype(jnp.float32) * deriv
            E[pl.ds(pl.multiple_of(t * TOK + m * MB, MB), MB), 0:cw] = eff.astype(jnp.bfloat16)
            return carry

        lax.fori_loop(0, 4 * steps, step, 0)

    back_in = {}

    def compute(n):
        c0, cw = CHUNKS[n]
        arrive(over_in[n])
        forward(n)
        steps = HALF // GM
        if n in G_OVER_LAST:
            prepare_side(n, 0)
            prepare_side(n, 1)
        else:
            back_in[n] = remote(
                G.at[pl.ds(pl.multiple_of((1 - h) * HALF, 16), HALF), pl.ds(c0, cw)],
                RY.at[:, pl.ds(c0, cw)], d_s.at[n], d_r.at[n], over,
            )
            sent.append(back_in[n])

        def step(k, carry):
            own_half = lax.div(k, steps)
            half = (1 - h) * (1 - own_half) + h * own_half
            part = pl.ds(pl.multiple_of(half * HALF + lax.rem(k, steps) * GM, GM), GM)
            acc = jnp.dot(XT[part, :], E[:, 0:cw], preferred_element_type=jnp.float32)
            G[part, c0 : c0 + cw] = acc.astype(jnp.bfloat16)
            if n in G_OVER_LAST:
                pl.when(k == steps - 1)(lambda: start_side(n, 1 - h, 0))
            else:
                pl.when(k == steps - 1)(back_in[n].start)
            return carry

        lax.fori_loop(0, 2 * steps, step, 0)
        if n in G_OVER_LAST:
            start_side(n, h, 1)

    sums_in = {}

    def start_side(n, hh, j):
        c0, cw = CHUNKS[n]
        cols = pl.ds(c0, cw)
        for i, d in enumerate(DIST):
            for pp in range(4):
                remote(
                    G.at[rows(hh, pp, ahead(q, d)), cols],
                    RX.at[i, pl.ds((4 * j + pp) * ROWS, ROWS), cols],
                    e_s.at[n, 3 * j + i], e_r.at[n, 3 * j + i], side[i],
                ).start()

    def prepare_side(n, j):
        c0, cw = CHUNKS[n]
        totals = []
        for i in range(3):
            whole = RX.at[i, pl.ds(4 * ROWS * j, 4 * ROWS), pl.ds(c0, cw)]
            totals.append(remote(whole, whole, e_s.at[n, 3 * j + i], e_r.at[n, 3 * j + i], side[i]))
        sums_in[n, j] = totals
        sent.extend(totals)

    def reduce_over(n):
        c0, cw = CHUNKS[n]
        back_in[n].wait_recv()

        def step(m, carry):
            here = pl.ds(pl.multiple_of(h * HALF + m * 256, 256), 256)
            there = pl.ds(pl.multiple_of(m * 256, 256), 256)
            total = G[here, c0 : c0 + cw].astype(jnp.float32) + RY[there, c0 : c0 + cw].astype(jnp.float32)
            G[here, c0 : c0 + cw] = total.astype(jnp.bfloat16)
            return carry

        lax.fori_loop(0, HALF // 256, step, 0)
        prepare_side(n, 0)
        start_side(n, h, 0)

    def side_sum(n, hh, first, target):
        c0, cw = CHUNKS[n]

        def step(pp, carry):
            part = pl.ds(pl.multiple_of(first + pp * ROWS, 16), ROWS)
            total = G[rows(hh, pp, q), c0 : c0 + cw].astype(jnp.float32)
            for i in range(3):
                total += RX[i, part, c0 : c0 + cw].astype(jnp.float32)
            target[pl.ds(pl.multiple_of(pp * ROWS, 16), ROWS), c0 : c0 + cw] = total.astype(jnp.bfloat16)
            return carry

        lax.fori_loop(0, 4, step, 0)

    last_in = []

    def finish(n):
        c0, cw = CHUNKS[n]
        there = out_hbm.at[0, :, quarter(p, c0, cw)]
        copies = []
        for i, d in enumerate(DIST):
            part = pl.ds(pl.multiple_of(ahead(p, d) * ROWS, 16), ROWS)
            copy = remote(T.at[part, pl.ds(c0, cw)], there, f_s.at[n, i], f_r.at[n, i], near[i])
            copy.start()
            copies.append(copy)
        part = pl.ds(pl.multiple_of(p * ROWS, 16), ROWS)
        mine = pltpu.make_async_copy(T.at[part, pl.ds(c0, cw)], there, own_sem.at[4 + n])
        mine.start()
        own.append(mine)
        last_in.append(copies)
        sent.extend(copies)

    def reduce_side(n):
        arrive(sums_in[n, 0])
        side_sum(n, h, 0, T)
        finish(n)

    def reduce_far_plane(n):
        arrive(sums_in[n, 0])
        side_sum(n, 1 - h, 0, T2)
        c0, cw = CHUNKS[n]
        cols = pl.ds(c0, cw)
        copy = remote(T2.at[:, cols], RY.at[pl.ds(0, 4 * ROWS), cols], d_s.at[n], d_r.at[n], over)
        copy.start()
        back_in[n] = copy
        sent.append(copy)

    def reduce_own_plane(n):
        arrive(sums_in[n, 1])
        side_sum(n, h, 4 * ROWS, T)

    def reduce_last(n):
        c0, cw = CHUNKS[n]
        back_in[n].wait_recv()

        def step(pp, carry):
            part = pl.ds(pl.multiple_of(pp * ROWS, 16), ROWS)
            total = T[part, c0 : c0 + cw].astype(jnp.float32) + RY[part, c0 : c0 + cw].astype(jnp.float32)
            T[part, c0 : c0 + cw] = total.astype(jnp.bfloat16)
            return carry

        lax.fori_loop(0, 4, step, 0)
        finish(n)

    late = {"compute": compute, "over": reduce_over, "side": reduce_side, "last": reduce_last}
    late.update({"drain": drain, "far_plane": reduce_far_plane, "own_plane": reduce_own_plane})
    late.update(early)
    for name, *which in LATE:
        late[name](*which)
    for copies in last_in:
        arrive(copies)
    drain()


def local(inputs, token_ids, upstream, weight, frag_index, global_params, local_params, momentum):
    n = len(CHUNKS)
    bf16, f32 = jnp.bfloat16, jnp.float32
    sems = [pltpu.SemaphoreType.DMA((4,))]
    sems += [pltpu.SemaphoreType.DMA((3,))] * 2
    sems += [pltpu.SemaphoreType.DMA((4 + 2 * n,))]
    for shape in ((2, 3), (3,), (4,), (n, 4), (n, 4), (n,), (n,), (n, 6), (n, 3), (n,), (n, 3), (n, 2)):
        sems += [pltpu.SemaphoreType.DMA(shape)] * 2
    hbm = pl.BlockSpec(memory_space=pltpu.HBM)
    span = global_params.shape[1]
    weight_grad, new_global, new_momentum = pl.pallas_call(
        kernel,
        name="inner_grad_outer_update",
        out_shape=(
            jax.ShapeDtypeStruct((1, ROWS, FW), bf16),
            jax.ShapeDtypeStruct((512, 128), f32),
            jax.ShapeDtypeStruct((512, 128), f32),
        ),
        in_specs=[hbm, hbm, hbm, hbm, pl.BlockSpec(memory_space=pltpu.SMEM), hbm, hbm, hbm],
        out_specs=[pl.BlockSpec(memory_space=pl.ANY)] * 3,
        scratch_shapes=[
            pltpu.VMEM((4, TOK, DW), bf16),
            pltpu.VMEM((DW, 4 * TOK), bf16),
            pltpu.VMEM((4, TOK, COLS), bf16),
            pltpu.VMEM((DW, COLS), bf16),
            pltpu.VMEM((4 * TOK, WIDE), bf16),
            pltpu.VMEM((DW, COLS), bf16),
            pltpu.VMEM((HALF, COLS), bf16),
            pltpu.VMEM((3, 8 * ROWS, COLS), bf16),
            pltpu.VMEM((4 * ROWS, COLS), bf16),
            pltpu.VMEM((4 * ROWS, COLS), bf16),
            pltpu.VMEM((4, ROWS, COLS), bf16),
            pltpu.VMEM((2, n, 256, WIDE), bf16),
            pltpu.VMEM((4, 8, TOK), f32),
            pltpu.VMEM((1, TOK), jnp.int32),
            pltpu.VMEM((16, span), f32),
            pltpu.VMEM((16, span), f32),
            pltpu.VMEM((16, span), f32),
            pltpu.VMEM((512, 128), f32),
            pltpu.VMEM((512, 128), f32),
            pltpu.VMEM((512, 128), bf16),
            pltpu.VMEM((256, 128), bf16),
            pltpu.VMEM((256, 128), bf16),
            pltpu.VMEM((256, 128), bf16),
            pltpu.VMEM((512, 128), f32),
            pltpu.VMEM((512, 128), f32),
            pltpu.VMEM((512, 128), f32),
            *sems,
        ],
        compiler_params=pltpu.CompilerParams(
            collective_id=0, has_side_effects=True, vmem_limit_bytes=53 * 2**20
        ),
        cost_estimate=pl.CostEstimate(
            flops=4 * TOK * DW * FW, bytes_accessed=22 * 2**20, transcendentals=TOK * FW
        ),
    )(inputs, token_ids, upstream, weight, frag_index, global_params, local_params, momentum)
    return (weight_grad, new_global.reshape(span), new_momentum.reshape(span))


def solution(mesh):
    placed = (
        P("replica", "fsdp", None),
        P("replica", "fsdp"),
        P("replica", "fsdp", None),
        P("replica", "fsdp", None),
        P(),
        P(None, "fsdp"),
        P("replica", None, "fsdp"),
        P(None, "fsdp"),
    )
    return jax.shard_map(
        local,
        mesh=mesh,
        in_specs=placed,
        out_specs=(P("replica", "fsdp", None), P("fsdp"), P("fsdp")),
        check_vma=False,
    )
```

```python
import functools

import jax
import jax.numpy as jnp
from jax import lax
from jax.experimental import pallas as pl
from jax.experimental.pallas import tpu as pltpu
from jax.sharding import PartitionSpec as P

MESH = pl.DeviceIdType.MESH
TOK, DW, FW = 512, 1536, 6144
ROWS = 48
HALF = 768
COLS = 1536
WIDE = 256
CHUNKS = tuple((c, WIDE) for c in range(0, COLS, WIDE))
FIRST = ((0, WIDE), (WIDE, COLS - WIDE))
W_OVER_FIRST = (5,)
G_OVER_LAST = (4, 5)
DIST = (1, 3, 2)
B_DIRECT = (0,)
EARLY = (
    ("send_up", 0), ("weight_ready", 0), ("to_side", 0), ("weight_ready", 1), ("to_side", 1), ("to_side", 2),
    ("to_near_again", 5), ("pick",), ("pass_side", 1), ("to_over", 0), ("to_side", 3), ("pass_side", 2),
    ("to_over", 1), ("to_side", 4), ("turn_own",), ("pass_side", 3), ("to_over", 2), ("pair",), ("pass_side", 4),
    ("up_own",), ("forward", 0, 1), ("pass_on", 0), ("pass_on", 1), ("to_over", 3), ("pass_up", 0), ("send_up", 1),
    ("send_up", 2), ("to_side_again", 5), ("to_over", 4), ("turn_near", 0), ("turn_near", 1), ("forward", 0, 3),
    ("forward", 1, 1), ("turn_far",), ("pass_up", 1), ("send_up", 3),
)
LATE = (
    ("compute", 0), ("sum",), ("pass_side_again", 5), ("pass_up", 2), ("send_up", 4), ("compute", 1), ("update",),
    ("pass_up", 3), ("send_up", 5), ("compute", 2),
    ("pass_up", 4), ("over", 0), ("compute", 3), ("pass_up", 5), ("over", 1), ("side", 0), ("compute", 4),
    ("compute", 5), ("over", 2), ("far_plane", 4), ("side", 1), ("far_plane", 5), ("own_plane", 4), ("over", 3),
    ("side", 2), ("own_plane", 5), ("last", 4), ("last", 5), ("side", 3),
)
MB = 512
GM = 384


def kernel(
    x_hbm, ids_hbm, up_hbm, w_hbm, frag_ref, gp_hbm, lp_hbm, mo_hbm,
    out_hbm, new_global, new_momentum,
    X, XT, U, W, G, RY, RX, T, T2, WY, UR, K, IDS,
    GP, LP, MO, CHOSEN, MOMENT, DIFF, DPAIR, PAIR, OTHER, DELTA,
    NEW_G, NEW_M, plan_sem, o_s, o_r, own_sem, a_s, a_r, k_s, k_r, x_s, x_r, u_s, u_r,
    b_s, b_r, c_s, c_r, d_s, d_r, e_s, e_r, f_s, f_r,
    v_s, v_r, g_s, g_r, r_r,
):
    ids_in = pltpu.make_async_copy(ids_hbm, IDS, plan_sem.at[3])
    ids_in.start()
    replica = lax.axis_index("replica")
    core, low = lax.rem(replica, 2), lax.div(replica, 2)
    me = lax.axis_index("fsdp")
    h, z, x = lax.div(me, 16), lax.rem(lax.div(me, 4), 4), lax.rem(me, 4)
    p = z + core * (x - z)
    q = x + core * (z - x)

    def place(hh, pp, qq):
        return hh * 16 + (pp + core * (qq - pp)) * 4 + (qq + core * (pp - qq))

    def rows(hh, pp, qq):
        return pl.ds(pl.multiple_of(place(hh, pp, qq) * ROWS, 16), ROWS)

    def dist(i):
        return 1 + 2 * i - 3 * lax.div(i, 2)

    def ahead(a, d):
        return lax.rem(a + d, 4)

    def remote(src, dst, send, recv, device, axis="fsdp"):
        return pltpu.make_async_remote_copy(
            src_ref=src, dst_ref=dst, send_sem=send, recv_sem=recv,
            device_id={axis: device}, device_id_type=MESH,
        )

    own, sent = [], []

    def drain():
        for mine in own:
            mine.wait()
        for copy in sent:
            copy.wait_send()
        own.clear()
        sent.clear()

    def quarter(pp, c0, cw):
        return pl.ds(pl.multiple_of(pp * COLS + c0, 128), cw)

    barrier = pltpu.get_barrier_semaphore()
    near = [place(h, ahead(p, d), q) for d in DIST]
    side = [place(h, p, ahead(q, d)) for d in DIST]
    over = place(1 - h, p, q)
    for device in near + side + [over]:
        pl.semaphore_signal(barrier, inc=1, device_id={"fsdp": device}, device_id_type=MESH)
    twin, mate = low * 2 + 1 - core, (1 - low) * 2 + core
    for device in (twin, mate):
        pl.semaphore_signal(barrier, inc=1, device_id={"replica": device}, device_id_type=MESH)
    pl.semaphore_wait(barrier, 9)

    weight_in = []
    for n, (c0, cw) in enumerate(FIRST):
        place_w = W.at[rows(h, p, q), pl.ds(c0, cw)]
        copies = []
        for i, d in enumerate(DIST):
            copy = remote(
                w_hbm.at[0, :, quarter(ahead(p, d), c0, cw)], place_w,
                a_s.at[n, i], a_r.at[n, i], near[i],
            )
            copy.start()
            copies.append(copy)
        mine = pltpu.make_async_copy(w_hbm.at[0, :, quarter(p, c0, cw)], place_w, own_sem.at[n])
        mine.start()
        weight_in.append((mine, copies))
        sent += copies

    cross_in = {}
    for n in W_OVER_FIRST:
        c0, cw = CHUNKS[n]
        cols = pl.ds(c0, cw)
        for pp in range(4):
            remote(w_hbm.at[0, :, quarter(pp, c0, cw)], WY.at[pp, :, cols], v_s.at[n], v_r.at[n], over).start()
        cross_in[n] = remote(WY.at[:, :, cols], WY.at[:, :, cols], v_s.at[n], v_r.at[n], over)
        sent.append(cross_in[n])

    ids_in.wait()
    K[p] = jnp.broadcast_to((IDS[...] != 0).astype(jnp.float32), (8, TOK))
    x_in, k_in, u_in = [], [], {}
    for i in range(2):
        x_in.append(remote(x_hbm.at[0], X.at[p], x_s.at[i], x_r.at[i], near[i]))
        x_in[i].start()
    x_own = pltpu.make_async_copy(x_hbm.at[0], X.at[p], own_sem.at[2])
    x_own.start()
    for i in range(3):
        k_in.append(remote(K.at[p], K.at[p], k_s.at[i], k_r.at[i], near[i]))
        k_in[i].start()

    relay_in = {}

    def send_up(n):
        c0, cw = CHUNKS[n]
        there = U.at[pl.ds(pl.multiple_of(p * TOK, TOK), TOK), pl.ds(c0, cw)]
        u_in[n], relay_in[n] = [], []
        far = quarter(ahead(p, 2), c0, cw)
        for i in range(2):
            copy = remote(
                up_hbm.at[0, :, quarter(ahead(p, DIST[i]), c0, cw)], there,
                u_s, u_r.at[n, i], near[i],
            )
            half = remote(up_hbm.at[0, pl.ds(256 * i, 256), far], UR.at[i, n], u_s, r_r.at[n, i], near[i])
            copy.start()
            half.start()
            u_in[n].append(copy)
            relay_in[n].append(half)

    def pass_up(n):
        c0, cw = CHUNKS[n]
        for i in range(2):
            relay_in[n][i].wait_recv()
            there = U.at[pl.ds(pl.multiple_of(blocks[i + 1] * TOK + 256 * i, 256), 256), pl.ds(c0, cw)]
            copy = remote(UR.at[i, n], there, u_s, u_r.at[n, 2 + i], near[i])
            copy.start()
            u_in[n].append(copy)

    u_own = pltpu.make_async_copy(
        up_hbm.at[0, :, quarter(p, 0, COLS)], U.at[pl.ds(pl.multiple_of(p * TOK, TOK), TOK)], own_sem.at[3]
    )
    u_own.start()
    blocks = [p] + [lax.rem(p - d + 4, 4) for d in DIST]

    def pass_on(i):
        x_in[i].wait_recv()
        part = X.at[blocks[i + 1], pl.ds(256 * i, 256)]
        x_in.append(remote(part, part, x_s.at[2 + i], x_r.at[2 + i], near[i]))
        x_in[2 + i].start()
        sent.append(x_in[2 + i])

    sent += x_in + k_in
    plan_in = []
    for i, (source, target) in enumerate(((gp_hbm, GP), (lp_hbm.at[0], LP), (mo_hbm, MO))):
        plan_in.append(pltpu.make_async_copy(source, target, plan_sem.at[i]))
        plan_in[i].start()

    mine_half = pl.ds(pl.multiple_of(core * 256, 16), 256)
    twin_half = pl.ds(pl.multiple_of((1 - core) * 256, 16), 256)
    pair_in = remote(DIFF.at[twin_half], DPAIR, o_s.at[0], o_r.at[0], twin, "replica")
    other_in = remote(PAIR, OTHER, o_s.at[1], o_r.at[1], mate, "replica")
    delta_in = remote(DELTA.at[mine_half], DELTA.at[mine_half], o_s.at[2], o_r.at[2], twin, "replica")
    sent += [pair_in, other_in, delta_in]

    def plan_pick():
        for copy in plan_in:
            copy.wait()
        fragment = frag_ref[0]

        def step(j, carry):
            cols = pl.ds(pl.multiple_of(j * 2048, 2048), 2048)
            part = pl.ds(pl.multiple_of(j * 16, 16), 16)
            chosen = GP[pl.ds(fragment, 1), cols].reshape(16, 128)
            CHOSEN[part, :] = chosen
            MOMENT[part, :] = MO[pl.ds(fragment, 1), cols].reshape(16, 128)
            DIFF[part, :] = (chosen - LP[pl.ds(fragment, 1), cols].reshape(16, 128)).astype(jnp.bfloat16)
            return carry

        lax.fori_loop(0, 32, step, 0)
        pair_in.start()

    def plan_pair():
        pair_in.wait_recv()
        PAIR[...] = (DIFF[mine_half, :].astype(jnp.float32) + DPAIR[...].astype(jnp.float32)).astype(jnp.bfloat16)
        other_in.start()

    def plan_sum():
        other_in.wait_recv()
        total = PAIR[...].astype(jnp.float32) + OTHER[...].astype(jnp.float32)
        DELTA[mine_half, :] = total * 0.25
        delta_in.start()

    def plan_update():
        delta_in.wait_recv()
        delta = DELTA[...]
        moment = 0.9 * MOMENT[...] + delta
        NEW_M[...] = moment
        NEW_G[...] = CHOSEN[...] - 0.7 * (delta + 0.9 * moment)
        for i, (source, target) in enumerate(((NEW_G, new_global), (NEW_M, new_momentum))):
            copy = pltpu.make_async_copy(source, target, plan_sem.at[i])
            copy.start()
            own.append(copy)

    def arrive(copies):
        for copy in copies:
            copy.wait_recv()

    side_in = {}

    def planes(n):
        return range(2) if n in W_OVER_FIRST else [h]

    def to_side(n):
        c0, cw = CHUNKS[n]
        cols = pl.ds(c0, cw)
        both = len(planes(n))
        count = 3 if n in B_DIRECT else 2

        def step(k, carry):
            i, hh, pp = lax.div(k, 4 * both), lax.rem(lax.div(k, 4), both), lax.rem(k, 4)
            part = W.at[rows(hh if both == 2 else h, pp, q), cols]
            remote(part, part, b_s, b_r.at[n, i], place(h, p, ahead(q, dist(i)))).start()
            return carry

        lax.fori_loop(0, 4 * both * count, step, 0)
        whole = W.at[pl.ds(0, 4 * ROWS * both), cols]
        side_in[n] = [remote(whole, whole, b_s, b_r.at[n, i], side[i]) for i in range(count)]

    def pass_side(n):
        c0, cw = CHUNKS[n]
        cols = pl.ds(c0, cw)
        both = len(planes(n))
        whole = W.at[pl.ds(0, 2 * ROWS * both), cols]
        for i in range(2):
            side_in[n][i].wait_recv()

            def step(k, carry, i=i):
                hh, pp = lax.div(k, 2), 2 * i + lax.rem(k, 2)
                part = W.at[rows(hh if both == 2 else h, pp, lax.rem(q - DIST[i] + 4, 4)), cols]
                remote(part, part, b_s, b_r.at[n, 2 + i], side[i]).start()
                return carry

            lax.fori_loop(0, 2 * both, step, 0)
            side_in[n].append(remote(whole, whole, b_s, b_r.at[n, 2 + i], side[i]))

    over_in = {}

    def to_over(n):
        arrive(side_in[n] if n in B_DIRECT else side_in[n][2:])
        c0, cw = CHUNKS[n]
        half = W.at[pl.ds(pl.multiple_of(h * HALF, 16), HALF), pl.ds(c0, cw)]
        copy = remote(half, half, c_s.at[n], c_r.at[n], over)
        copy.start()
        over_in[n] = [copy]
        sent.append(copy)

    again_in = {}

    def to_near_again(n):
        cross_in[n].wait_recv()
        c0, cw = CHUNKS[n]
        cols = pl.ds(c0, cw)
        there = W.at[rows(1 - h, p, q), cols]
        copies = []
        for i, d in enumerate(DIST):
            copies.append(remote(WY.at[ahead(p, d), :, cols], there, g_s.at[n, i], g_r.at[n, i], near[i]))
            copies[i].start()
        mine = pltpu.make_async_copy(WY.at[p, :, cols], there, own_sem.at[4 + len(CHUNKS) + n])
        mine.start()
        again_in[n] = (mine, copies)
        sent.extend(copies)

    def to_side_again(n):
        again_in[n][0].wait()
        arrive(again_in[n][1])
        to_side(n)

    def pass_side_again(n):
        pass_side(n)
        over_in[n] = side_in[n][2:]

    def turn(t):
        kept = K[t][0:1, :].astype(jnp.bfloat16)

        def step(j, carry):
            cols = pl.ds(pl.multiple_of(j * 256, 256), 256)
            XT[cols, pl.ds(pl.multiple_of(t * TOK, TOK), TOK)] = jnp.transpose(X[t, :, cols]) * kept
            return carry

        lax.fori_loop(0, DW // 256, step, 0)

    def weight_ready(n):
        weight_in[n][0].wait()
        arrive(weight_in[n][1])

    def turn_own():
        x_own.wait()
        turn(p)

    def turn_near(i):
        k_in[i].wait_recv()
        turn(blocks[i + 1])

    def turn_far():
        k_in[2].wait_recv()
        x_in[2].wait_recv()
        x_in[3].wait_recv()
        turn(blocks[3])

    def effect(t, m, c):
        part = pl.ds(pl.multiple_of(m * MB, MB), MB)
        cols = pl.ds(pl.multiple_of(c * WIDE, WIDE), WIDE)
        pre = jnp.dot(X[t, part, :], W[:, cols], preferred_element_type=jnp.float32)
        sig = 0.5 + 0.5 * jnp.tanh(0.5 * pre)
        deriv = sig * (1.0 + pre * (1.0 - sig))
        here = pl.ds(pl.multiple_of(t * TOK + m * MB, MB), MB)
        U[here, cols] = (U[here, cols].astype(jnp.float32) * deriv).astype(jnp.bfloat16)

    steps_in = TOK // MB
    done = {n: 0 for n in range(len(CHUNKS))}

    def forward(n, last):
        first = done[n]
        done[n] = last
        if first == 0:
            arrive(over_in[n])

        def step(k, carry):
            b, m = lax.div(k, steps_in), lax.rem(k, steps_in)
            for i in range(2):
                if first <= i + 1 < last:
                    pl.when(k == (i + 1) * steps_in)(u_in[n][i].wait_recv)
            if last == 4:
                pl.when(k == 3 * steps_in)(lambda: arrive(u_in[n][2:]))
            t = lax.rem(p - (b + lax.div(b, 2) - 2 * lax.div(b, 3)) + 4, 4)
            effect(t, m, n)
            return carry

        lax.fori_loop(first * steps_in, last * steps_in, step, 0)

    early = {
        "weight_ready": weight_ready, "to_side": to_side, "to_near_again": to_near_again, "to_over": to_over,
        "to_side_again": to_side_again, "send_up": send_up, "pass_on": pass_on, "pass_up": pass_up, "pass_side": pass_side, "pass_side_again": pass_side_again, "turn_own": turn_own,
        "turn_near": turn_near, "turn_far": turn_far, "pick": plan_pick, "pair": plan_pair, "sum": plan_sum,
        "update": plan_update, "up_own": u_own.wait, "forward": forward,
    }
    for name, *which in EARLY:
        early[name](*which)

    back_in = {}

    def compute(n):
        c0, cw = CHUNKS[n]
        forward(n, 4)
        steps = HALF // GM
        if n in G_OVER_LAST:
            prepare_side(n, 0)
            prepare_side(n, 1)
        else:
            back_in[n] = remote(
                G.at[pl.ds(pl.multiple_of((1 - h) * HALF, 16), HALF), pl.ds(c0, cw)],
                RY.at[:, pl.ds(c0, cw)], d_s.at[n], d_r.at[n], over,
            )
            sent.append(back_in[n])

        def step(k, carry):
            own_half = lax.div(k, steps)
            half = (1 - h) * (1 - own_half) + h * own_half
            part = pl.ds(pl.multiple_of(half * HALF + lax.rem(k, steps) * GM, GM), GM)
            acc = jnp.dot(XT[part, :], U[:, c0 : c0 + cw], preferred_element_type=jnp.float32)
            G[part, c0 : c0 + cw] = acc.astype(jnp.bfloat16)
            if n in G_OVER_LAST:
                pl.when(k == steps - 1)(lambda: start_side(n, 1 - h, 0))
            else:
                pl.when(k == steps - 1)(back_in[n].start)
            return carry

        lax.fori_loop(0, 2 * steps, step, 0)
        if n in G_OVER_LAST:
            start_side(n, h, 1)

    sums_in = {}

    def start_side(n, hh, j):
        c0, cw = CHUNKS[n]
        cols = pl.ds(c0, cw)

        def step(k, carry):
            i, pp = lax.div(k, 4), lax.rem(k, 4)
            to = ahead(q, dist(i))
            remote(
                G.at[rows(hh, pp, to), cols],
                RX.at[i, pl.ds(pl.multiple_of((4 * j + pp) * ROWS, 16), ROWS), cols],
                e_s, e_r.at[n, 3 * j + i], place(h, p, to),
            ).start()
            return carry

        lax.fori_loop(0, 12, step, 0)

    def prepare_side(n, j):
        c0, cw = CHUNKS[n]
        whole = RX.at[0, pl.ds(4 * ROWS * j, 4 * ROWS), pl.ds(c0, cw)]
        sums_in[n, j] = [remote(whole, whole, e_s, e_r.at[n, 3 * j + i], side[i]) for i in range(3)]

    def reduce_over(n):
        c0, cw = CHUNKS[n]
        back_in[n].wait_recv()

        def step(m, carry):
            here = pl.ds(pl.multiple_of(h * HALF + m * 256, 256), 256)
            there = pl.ds(pl.multiple_of(m * 256, 256), 256)
            total = G[here, c0 : c0 + cw].astype(jnp.float32) + RY[there, c0 : c0 + cw].astype(jnp.float32)
            G[here, c0 : c0 + cw] = total.astype(jnp.bfloat16)
            return carry

        lax.fori_loop(0, HALF // 256, step, 0)
        prepare_side(n, 0)
        start_side(n, h, 0)

    def side_sum(n, hh, first, target):
        c0, cw = CHUNKS[n]

        def step(pp, carry):
            part = pl.ds(pl.multiple_of(first + pp * ROWS, 16), ROWS)
            total = G[rows(hh, pp, q), c0 : c0 + cw].astype(jnp.float32)
            for i in range(3):
                total += RX[i, part, c0 : c0 + cw].astype(jnp.float32)
            target[pl.ds(pl.multiple_of(pp * ROWS, 16), ROWS), c0 : c0 + cw] = total.astype(jnp.bfloat16)
            return carry

        lax.fori_loop(0, 4, step, 0)

    def finish(n):
        c0, cw = CHUNKS[n]
        there = out_hbm.at[0, :, quarter(p, c0, cw)]

        def step(i, carry):
            to = ahead(p, dist(i))
            part = pl.ds(pl.multiple_of(to * ROWS, 16), ROWS)
            remote(T.at[part, pl.ds(c0, cw)], there, f_s, f_r, place(h, to, q)).start()
            return carry

        lax.fori_loop(0, 3, step, 0)
        part = pl.ds(pl.multiple_of(p * ROWS, 16), ROWS)
        mine = pltpu.make_async_copy(T.at[part, pl.ds(c0, cw)], there, own_sem.at[4 + n])
        mine.start()
        own.append(mine)

    def reduce_side(n):
        arrive(sums_in[n, 0])
        side_sum(n, h, 0, T)
        finish(n)

    def reduce_far_plane(n):
        arrive(sums_in[n, 0])
        side_sum(n, 1 - h, 0, T2)
        c0, cw = CHUNKS[n]
        cols = pl.ds(c0, cw)
        copy = remote(T2.at[:, cols], RY.at[pl.ds(0, 4 * ROWS), cols], d_s.at[n], d_r.at[n], over)
        copy.start()
        back_in[n] = copy
        sent.append(copy)

    def reduce_own_plane(n):
        arrive(sums_in[n, 1])
        side_sum(n, h, 4 * ROWS, T)

    def reduce_last(n):
        c0, cw = CHUNKS[n]
        back_in[n].wait_recv()

        def step(pp, carry):
            part = pl.ds(pl.multiple_of(pp * ROWS, 16), ROWS)
            total = T[part, c0 : c0 + cw].astype(jnp.float32) + RY[part, c0 : c0 + cw].astype(jnp.float32)
            T[part, c0 : c0 + cw] = total.astype(jnp.bfloat16)
            return carry

        lax.fori_loop(0, 4, step, 0)
        finish(n)

    late = {"compute": compute, "over": reduce_over, "side": reduce_side, "last": reduce_last}
    late.update({"drain": drain, "far_plane": reduce_far_plane, "own_plane": reduce_own_plane})
    late.update(early)
    for name, *which in LATE:
        late[name](*which)
    total = T.at[pl.ds(0, 3 * len(CHUNKS) * ROWS * WIDE // COLS)]
    all_f = remote(total, total, f_s, f_r, near[0])
    all_f.wait_recv()
    units = 12 * ROWS * WIDE // COLS
    total = W.at[pl.ds(0, units * (len(CHUNKS) + len(W_OVER_FIRST)))]
    all_b = remote(total, total, b_s, f_r, near[0])
    total = G.at[pl.ds(0, units * (len(CHUNKS) + len(G_OVER_LAST)))]
    all_e = remote(total, total, e_s, f_r, near[0])
    sent.extend([all_f, all_b, all_e, remote(U, U, u_s, f_r, near[0])])
    drain()


def local(inputs, token_ids, upstream, weight, frag_index, global_params, local_params, momentum):
    n = len(CHUNKS)
    bf16, f32 = jnp.bfloat16, jnp.float32
    dma = pltpu.SemaphoreType.DMA
    sems = [dma((4,)), dma((3,)), dma((3,)), dma((4 + 2 * n,))]
    for send, receive in (
        ((2, 3), (2, 3)), ((3,), (3,)), ((4,), (4,)), ((), (n, 4)), ((), (n, 4)), ((n,), (n,)), ((n,), (n,)),
        ((), (n, 6)), ((), ()), ((n,), (n,)), ((n, 3), (n, 3)),
    ):
        sems += [dma(send), dma(receive)]
    sems.append(dma((n, 2)))
    hbm = pl.BlockSpec(memory_space=pltpu.HBM)
    span = global_params.shape[1]
    weight_grad, new_global, new_momentum = pl.pallas_call(
        kernel,
        name="inner_grad_outer_update",
        out_shape=(
            jax.ShapeDtypeStruct((1, ROWS, FW), bf16),
            jax.ShapeDtypeStruct((512, 128), f32),
            jax.ShapeDtypeStruct((512, 128), f32),
        ),
        in_specs=[hbm, hbm, hbm, hbm, pl.BlockSpec(memory_space=pltpu.SMEM), hbm, hbm, hbm],
        out_specs=[pl.BlockSpec(memory_space=pl.ANY)] * 3,
        scratch_shapes=[
            pltpu.VMEM((4, TOK, DW), bf16),
            pltpu.VMEM((DW, 4 * TOK), bf16),
            pltpu.VMEM((4 * TOK, COLS), bf16),
            pltpu.VMEM((DW, COLS), bf16),
            pltpu.VMEM((DW, COLS), bf16),
            pltpu.VMEM((HALF, COLS), bf16),
            pltpu.VMEM((3, 8 * ROWS, COLS), bf16),
            pltpu.VMEM((4 * ROWS, COLS), bf16),
            pltpu.VMEM((4 * ROWS, COLS), bf16),
            pltpu.VMEM((4, ROWS, COLS), bf16),
            pltpu.VMEM((2, n, 256, WIDE), bf16),
            pltpu.VMEM((4, 8, TOK), f32),
            pltpu.VMEM((1, TOK), jnp.int32),
            pltpu.VMEM((16, span), f32),
            pltpu.VMEM((16, span), f32),
            pltpu.VMEM((16, span), f32),
            pltpu.VMEM((512, 128), f32),
            pltpu.VMEM((512, 128), f32),
            pltpu.VMEM((512, 128), bf16),
            pltpu.VMEM((256, 128), bf16),
            pltpu.VMEM((256, 128), bf16),
            pltpu.VMEM((256, 128), bf16),
            pltpu.VMEM((512, 128), f32),
            pltpu.VMEM((512, 128), f32),
            pltpu.VMEM((512, 128), f32),
            *sems,
        ],
        compiler_params=pltpu.CompilerParams(
            collective_id=0, has_side_effects=True, vmem_limit_bytes=53 * 2**20
        ),
        cost_estimate=pl.CostEstimate(
            flops=4 * TOK * DW * FW, bytes_accessed=22 * 2**20, transcendentals=TOK * FW
        ),
    )(inputs, token_ids, upstream, weight, frag_index, global_params, local_params, momentum)
    return (weight_grad, new_global.reshape(span), new_momentum.reshape(span))


def solution(mesh):
    placed = (
        P("replica", "fsdp", None),
        P("replica", "fsdp"),
        P("replica", "fsdp", None),
        P("replica", "fsdp", None),
        P(),
        P(None, "fsdp"),
        P("replica", None, "fsdp"),
        P(None, "fsdp"),
    )
    return jax.shard_map(
        local,
        mesh=mesh,
        in_specs=placed,
        out_specs=(P("replica", "fsdp", None), P("fsdp"), P("fsdp")),
        check_vma=False,
    )
```

```python
import functools

import jax
import jax.numpy as jnp
from jax import lax
from jax.experimental import pallas as pl
from jax.experimental.pallas import tpu as pltpu
from jax.sharding import PartitionSpec as P

MESH = pl.DeviceIdType.MESH
TOK, DW, FW = 512, 1536, 6144
ROWS = 48
HALF = 768
COLS = 1536
WIDE = 256
CHUNKS = tuple((c, WIDE) for c in range(0, COLS, WIDE))
FIRST = ((0, WIDE), (WIDE, COLS - WIDE))
W_OVER_FIRST = (5,)
G_OVER_LAST = (4, 5)
DIST = (1, 3, 2)
B_DIRECT = (0,)
EARLY = (
    ("send_up", 0), ("weight_ready", 0), ("to_side", 0), ("weight_ready", 1), ("to_side", 1), ("to_side", 2),
    ("to_near_again", 5), ("pick",), ("pass_side", 1), ("to_over", 0), ("to_side", 3), ("pass_side", 2),
    ("to_over", 1), ("to_side", 4), ("turn_own",), ("pass_side", 3), ("to_over", 2), ("pair",), ("pass_side", 4),
    ("up_own",), ("forward", 0, 1), ("pass_on", 0), ("pass_on", 1), ("to_over", 3), ("pass_up", 0), ("send_up", 1),
    ("send_up", 2), ("to_side_again", 5), ("to_over", 4), ("turn_near", 0), ("turn_near", 1), ("forward", 0, 3),
    ("forward", 1, 1), ("turn_far",), ("pass_up", 1), ("send_up", 3),
)
LATE = (
    ("compute", 0), ("sum",), ("pass_side_again", 5), ("pass_up", 2), ("send_up", 4), ("compute", 1), ("update",),
    ("pass_up", 3), ("send_up", 5), ("compute", 2),
    ("pass_up", 4), ("over", 0), ("compute", 3), ("pass_up", 5), ("over", 1), ("side", 0), ("compute", 4),
    ("compute", 5), ("over", 2), ("far_plane", 4), ("side", 1), ("far_plane", 5), ("own_plane", 4), ("over", 3),
    ("side", 2), ("own_plane", 5), ("last", 4), ("last", 5), ("side", 3),
)
MB = 512
GM = 384


def kernel(
    x_hbm, ids_hbm, up_hbm, w_hbm, frag_ref, gp_hbm, lp_hbm, mo_hbm,
    out_hbm, new_global, new_momentum,
    X, XT, U, W, G, RY, RX, T, T2, TY, WY, UR, K, IDS,
    GP, LP, MO, CHOSEN, MOMENT, DIFF, DPAIR, PAIR, OTHER, DELTA,
    NEW_G, NEW_M, plan_sem, o_s, o_r, own_sem, a_s, a_r, k_s, k_r, x_s, x_r, u_s, u_r,
    b_s, b_r, c_s, c_r, d_s, d_r, e_s, e_r, f_s, f_r,
    v_s, v_r, g_s, g_r, r_r,
):
    ids_in = pltpu.make_async_copy(ids_hbm, IDS, plan_sem.at[3])
    ids_in.start()
    replica = lax.axis_index("replica")
    core, low = lax.rem(replica, 2), lax.div(replica, 2)
    me = lax.axis_index("fsdp")
    h, z, x = lax.div(me, 16), lax.rem(lax.div(me, 4), 4), lax.rem(me, 4)
    p = z + core * (x - z)
    q = x + core * (z - x)

    def place(hh, pp, qq):
        return hh * 16 + (pp + core * (qq - pp)) * 4 + (qq + core * (pp - qq))

    def rows(hh, pp, qq):
        return pl.ds(pl.multiple_of(place(hh, pp, qq) * ROWS, 16), ROWS)

    def dist(i):
        return 1 + 2 * i - 3 * lax.div(i, 2)

    def ahead(a, d):
        return lax.rem(a + d, 4)

    def remote(src, dst, send, recv, device, axis="fsdp"):
        return pltpu.make_async_remote_copy(
            src_ref=src, dst_ref=dst, send_sem=send, recv_sem=recv,
            device_id={axis: device}, device_id_type=MESH,
        )

    own, sent = [], []

    def drain():
        for mine in own:
            mine.wait()
        for copy in sent:
            copy.wait_send()
        own.clear()
        sent.clear()

    def quarter(pp, c0, cw):
        return pl.ds(pl.multiple_of(pp * COLS + c0, 128), cw)

    barrier = pltpu.get_barrier_semaphore()
    near = [place(h, ahead(p, d), q) for d in DIST]
    side = [place(h, p, ahead(q, d)) for d in DIST]
    over = place(1 - h, p, q)
    for device in near + side + [over]:
        pl.semaphore_signal(barrier, inc=1, device_id={"fsdp": device}, device_id_type=MESH)
    twin, mate = low * 2 + 1 - core, (1 - low) * 2 + core
    for device in (twin, mate):
        pl.semaphore_signal(barrier, inc=1, device_id={"replica": device}, device_id_type=MESH)
    pl.semaphore_wait(barrier, 9)

    weight_in = []
    for n, (c0, cw) in enumerate(FIRST):
        place_w = W.at[rows(h, p, q), pl.ds(c0, cw)]
        copies = []
        for i, d in enumerate(DIST):
            copy = remote(
                w_hbm.at[0, :, quarter(ahead(p, d), c0, cw)], place_w,
                a_s.at[n, i], a_r.at[n, i], near[i],
            )
            copy.start()
            copies.append(copy)
        mine = pltpu.make_async_copy(w_hbm.at[0, :, quarter(p, c0, cw)], place_w, own_sem.at[n])
        mine.start()
        weight_in.append((mine, copies))
        sent += copies

    cross_in = {}
    for n in W_OVER_FIRST:
        c0, cw = CHUNKS[n]
        cols = pl.ds(c0, cw)
        for pp in range(4):
            remote(w_hbm.at[0, :, quarter(pp, c0, cw)], WY.at[pp, :, cols], v_s.at[n], v_r.at[n], over).start()
        cross_in[n] = remote(WY.at[:, :, cols], WY.at[:, :, cols], v_s.at[n], v_r.at[n], over)
        sent.append(cross_in[n])

    ids_in.wait()
    K[p] = jnp.broadcast_to((IDS[...] != 0).astype(jnp.float32), (8, TOK))
    x_in, k_in, u_in = [], [], {}
    for i in range(2):
        x_in.append(remote(x_hbm.at[0], X.at[p], x_s.at[i], x_r.at[i], near[i]))
        x_in[i].start()
    x_own = pltpu.make_async_copy(x_hbm.at[0], X.at[p], own_sem.at[2])
    x_own.start()
    for i in range(3):
        k_in.append(remote(K.at[p], K.at[p], k_s.at[i], k_r.at[i], near[i]))
        k_in[i].start()

    relay_in = {}

    def send_up(n):
        c0, cw = CHUNKS[n]
        there = U.at[pl.ds(pl.multiple_of(p * TOK, TOK), TOK), pl.ds(c0, cw)]
        u_in[n], relay_in[n] = [], []
        far = quarter(ahead(p, 2), c0, cw)
        for i in range(2):
            copy = remote(
                up_hbm.at[0, :, quarter(ahead(p, DIST[i]), c0, cw)], there,
                u_s, u_r.at[n, i], near[i],
            )
            half = remote(up_hbm.at[0, pl.ds(256 * i, 256), far], UR.at[i, n], u_s, r_r.at[n, i], near[i])
            copy.start()
            half.start()
            u_in[n].append(copy)
            relay_in[n].append(half)

    def pass_up(n):
        c0, cw = CHUNKS[n]
        for i in range(2):
            relay_in[n][i].wait_recv()
            there = U.at[pl.ds(pl.multiple_of(blocks[i + 1] * TOK + 256 * i, 256), 256), pl.ds(c0, cw)]
            copy = remote(UR.at[i, n], there, u_s, u_r.at[n, 2 + i], near[i])
            copy.start()
            u_in[n].append(copy)

    u_own = pltpu.make_async_copy(
        up_hbm.at[0, :, quarter(p, 0, COLS)], U.at[pl.ds(pl.multiple_of(p * TOK, TOK), TOK)], own_sem.at[3]
    )
    u_own.start()
    blocks = [p] + [lax.rem(p - d + 4, 4) for d in DIST]

    def pass_on(i):
        x_in[i].wait_recv()
        part = X.at[blocks[i + 1], pl.ds(256 * i, 256)]
        x_in.append(remote(part, part, x_s.at[2 + i], x_r.at[2 + i], near[i]))
        x_in[2 + i].start()
        sent.append(x_in[2 + i])

    sent += x_in + k_in
    plan_in = []
    for i, (source, target) in enumerate(((gp_hbm, GP), (lp_hbm.at[0], LP), (mo_hbm, MO))):
        plan_in.append(pltpu.make_async_copy(source, target, plan_sem.at[i]))
        plan_in[i].start()

    mine_half = pl.ds(pl.multiple_of(core * 256, 16), 256)
    twin_half = pl.ds(pl.multiple_of((1 - core) * 256, 16), 256)
    pair_in = remote(DIFF.at[twin_half], DPAIR, o_s.at[0], o_r.at[0], twin, "replica")
    other_in = remote(PAIR, OTHER, o_s.at[1], o_r.at[1], mate, "replica")
    delta_in = remote(DELTA.at[mine_half], DELTA.at[mine_half], o_s.at[2], o_r.at[2], twin, "replica")
    sent += [pair_in, other_in, delta_in]

    def plan_pick():
        for copy in plan_in:
            copy.wait()
        fragment = frag_ref[0]

        def step(j, carry):
            cols = pl.ds(pl.multiple_of(j * 2048, 2048), 2048)
            part = pl.ds(pl.multiple_of(j * 16, 16), 16)
            chosen = GP[pl.ds(fragment, 1), cols].reshape(16, 128)
            CHOSEN[part, :] = chosen
            MOMENT[part, :] = MO[pl.ds(fragment, 1), cols].reshape(16, 128)
            DIFF[part, :] = (chosen - LP[pl.ds(fragment, 1), cols].reshape(16, 128)).astype(jnp.bfloat16)
            return carry

        lax.fori_loop(0, 32, step, 0)
        pair_in.start()

    def plan_pair():
        pair_in.wait_recv()
        PAIR[...] = (DIFF[mine_half, :].astype(jnp.float32) + DPAIR[...].astype(jnp.float32)).astype(jnp.bfloat16)
        other_in.start()

    def plan_sum():
        other_in.wait_recv()
        total = PAIR[...].astype(jnp.float32) + OTHER[...].astype(jnp.float32)
        DELTA[mine_half, :] = total * 0.25
        delta_in.start()

    def plan_update():
        delta_in.wait_recv()
        delta = DELTA[...]
        moment = 0.9 * MOMENT[...] + delta
        NEW_M[...] = moment
        NEW_G[...] = CHOSEN[...] - 0.7 * (delta + 0.9 * moment)
        for i, (source, target) in enumerate(((NEW_G, new_global), (NEW_M, new_momentum))):
            copy = pltpu.make_async_copy(source, target, plan_sem.at[i])
            copy.start()
            own.append(copy)

    def arrive(copies):
        for copy in copies:
            copy.wait_recv()

    side_in = {}

    def planes(n):
        return range(2) if n in W_OVER_FIRST else [h]

    def to_side(n):
        c0, cw = CHUNKS[n]
        cols = pl.ds(c0, cw)
        both = len(planes(n))
        count = 3 if n in B_DIRECT else 2

        def step(k, carry):
            i, hh, pp = lax.div(k, 4 * both), lax.rem(lax.div(k, 4), both), lax.rem(k, 4)
            part = W.at[rows(hh if both == 2 else h, pp, q), cols]
            remote(part, part, b_s, b_r.at[n, i], place(h, p, ahead(q, dist(i)))).start()
            return carry

        lax.fori_loop(0, 4 * both * count, step, 0)
        whole = W.at[pl.ds(0, 4 * ROWS * both), cols]
        side_in[n] = [remote(whole, whole, b_s, b_r.at[n, i], side[i]) for i in range(count)]

    def pass_side(n):
        c0, cw = CHUNKS[n]
        cols = pl.ds(c0, cw)
        both = len(planes(n))
        whole = W.at[pl.ds(0, 2 * ROWS * both), cols]
        for i in range(2):
            side_in[n][i].wait_recv()

            def step(k, carry, i=i):
                hh, pp = lax.div(k, 2), 2 * i + lax.rem(k, 2)
                part = W.at[rows(hh if both == 2 else h, pp, lax.rem(q - DIST[i] + 4, 4)), cols]
                remote(part, part, b_s, b_r.at[n, 2 + i], side[i]).start()
                return carry

            lax.fori_loop(0, 2 * both, step, 0)
            side_in[n].append(remote(whole, whole, b_s, b_r.at[n, 2 + i], side[i]))

    over_in = {}

    def to_over(n):
        arrive(side_in[n] if n in B_DIRECT else side_in[n][2:])
        c0, cw = CHUNKS[n]
        half = W.at[pl.ds(pl.multiple_of(h * HALF, 16), HALF), pl.ds(c0, cw)]
        copy = remote(half, half, c_s.at[n], c_r.at[n], over)
        copy.start()
        over_in[n] = [copy]
        sent.append(copy)

    again_in = {}

    def to_near_again(n):
        cross_in[n].wait_recv()
        c0, cw = CHUNKS[n]
        cols = pl.ds(c0, cw)
        there = W.at[rows(1 - h, p, q), cols]
        copies = []
        for i, d in enumerate(DIST):
            copies.append(remote(WY.at[ahead(p, d), :, cols], there, g_s.at[n, i], g_r.at[n, i], near[i]))
            copies[i].start()
        mine = pltpu.make_async_copy(WY.at[p, :, cols], there, own_sem.at[4 + len(CHUNKS) + n])
        mine.start()
        again_in[n] = (mine, copies)
        sent.extend(copies)

    def to_side_again(n):
        again_in[n][0].wait()
        arrive(again_in[n][1])
        to_side(n)

    def pass_side_again(n):
        pass_side(n)
        over_in[n] = side_in[n][2:]

    def turn(t):
        kept = K[t][0:1, :].astype(jnp.bfloat16)

        def step(j, carry):
            cols = pl.ds(pl.multiple_of(j * 256, 256), 256)
            XT[cols, pl.ds(pl.multiple_of(t * TOK, TOK), TOK)] = jnp.transpose(X[t, :, cols]) * kept
            return carry

        lax.fori_loop(0, DW // 256, step, 0)

    def weight_ready(n):
        weight_in[n][0].wait()
        arrive(weight_in[n][1])

    def turn_own():
        x_own.wait()
        turn(p)

    def turn_near(i):
        k_in[i].wait_recv()
        turn(blocks[i + 1])

    def turn_far():
        k_in[2].wait_recv()
        x_in[2].wait_recv()
        x_in[3].wait_recv()
        turn(blocks[3])

    def effect(t, m, c):
        part = pl.ds(pl.multiple_of(m * MB, MB), MB)
        cols = pl.ds(pl.multiple_of(c * WIDE, WIDE), WIDE)
        pre = jnp.dot(X[t, part, :], W[:, cols], preferred_element_type=jnp.float32)
        sig = 0.5 + 0.5 * jnp.tanh(0.5 * pre)
        deriv = sig * (1.0 + pre * (1.0 - sig))
        here = pl.ds(pl.multiple_of(t * TOK + m * MB, MB), MB)
        U[here, cols] = (U[here, cols].astype(jnp.float32) * deriv).astype(jnp.bfloat16)

    steps_in = TOK // MB
    done = {n: 0 for n in range(len(CHUNKS))}

    def forward(n, last):
        first = done[n]
        done[n] = last
        if first == 0:
            arrive(over_in[n])

        def step(k, carry):
            b, m = lax.div(k, steps_in), lax.rem(k, steps_in)
            for i in range(2):
                if first <= i + 1 < last:
                    pl.when(k == (i + 1) * steps_in)(u_in[n][i].wait_recv)
            if last == 4:
                pl.when(k == 3 * steps_in)(lambda: arrive(u_in[n][2:]))
            t = lax.rem(p - (b + lax.div(b, 2) - 2 * lax.div(b, 3)) + 4, 4)
            effect(t, m, n)
            return carry

        lax.fori_loop(first * steps_in, last * steps_in, step, 0)

    early = {
        "weight_ready": weight_ready, "to_side": to_side, "to_near_again": to_near_again, "to_over": to_over,
        "to_side_again": to_side_again, "send_up": send_up, "pass_on": pass_on, "pass_up": pass_up, "pass_side": pass_side, "pass_side_again": pass_side_again, "turn_own": turn_own,
        "turn_near": turn_near, "turn_far": turn_far, "pick": plan_pick, "pair": plan_pair, "sum": plan_sum,
        "update": plan_update, "up_own": u_own.wait, "forward": forward,
    }
    for name, *which in EARLY:
        early[name](*which)

    back_in = {}

    def compute(n):
        c0, cw = CHUNKS[n]
        forward(n, 4)
        steps = HALF // GM
        if n in G_OVER_LAST:
            prepare_side(n, 0)
            prepare_side(n, 1)
        else:
            back_in[n] = remote(
                G.at[1 - h, :, :, :, pl.ds(c0, cw)], RY.at[:, :, :, pl.ds(c0, cw)], d_s.at[n], d_r.at[n], over,
            )
            sent.append(back_in[n])

        def step(k, carry):
            own_half = lax.div(k, steps)
            half = (1 - h) * (1 - own_half) + h * own_half
            part = pl.ds(pl.multiple_of(half * HALF + lax.rem(k, steps) * GM, GM), GM)
            acc = jnp.dot(XT[part, :], U[:, c0 : c0 + cw], preferred_element_type=jnp.float32)
            planes_z = pl.ds(lax.rem(k, steps) * (GM // 192), GM // 192)
            G[half, planes_z, :, :, c0 : c0 + cw] = acc.astype(jnp.bfloat16).reshape(GM // 192, 4, ROWS, cw)
            if n in G_OVER_LAST:
                pl.when(k == steps - 1)(lambda: start_side(n, 1 - h, 0))
            else:
                pl.when(k == steps - 1)(back_in[n].start)
            return carry

        lax.fori_loop(0, 2 * steps, step, 0)
        if n in G_OVER_LAST:
            start_side(n, h, 1)

    sums_in = {}

    def start_side(n, hh, j):
        c0, cw = CHUNKS[n]
        cols = pl.ds(c0, cw)

        def step(i, carry):
            to = ahead(q, dist(i))
            there = RX.at[i, pl.ds(4 * j, 4), :, cols]
            device = place(h, p, to)

            @pl.when(core == 0)
            def _():
                remote(G.at[hh, :, to, :, cols], there, e_s, e_r.at[n, 3 * j + i], device).start()

            @pl.when(core == 1)
            def _():
                remote(G.at[hh, to, :, :, cols], there, e_s, e_r.at[n, 3 * j + i], device).start()

            return carry

        lax.fori_loop(0, 3, step, 0)

    def prepare_side(n, j):
        c0, cw = CHUNKS[n]
        whole = RX.at[0, pl.ds(4 * j, 4), :, pl.ds(c0, cw)]
        sums_in[n, j] = [remote(whole, whole, e_s, e_r.at[n, 3 * j + i], side[i]) for i in range(3)]

    def reduce_over(n):
        c0, cw = CHUNKS[n]
        back_in[n].wait_recv()

        def step(m, carry):
            total = G[h, m, :, :, c0 : c0 + cw].astype(jnp.float32) + RY[m, :, :, c0 : c0 + cw].astype(jnp.float32)
            G[h, m, :, :, c0 : c0 + cw] = total.astype(jnp.bfloat16)
            return carry

        lax.fori_loop(0, 4, step, 0)
        prepare_side(n, 0)
        start_side(n, h, 0)

    def side_sum(n, hh, first, target):
        c0, cw = CHUNKS[n]

        def step(pp, carry):
            zz, xx = pp + core * (q - pp), q + core * (pp - q)
            total = G[hh, zz, xx, :, c0 : c0 + cw].astype(jnp.float32)
            for i in range(3):
                total += RX[i, first + pp, :, c0 : c0 + cw].astype(jnp.float32)
            target[pl.ds(pl.multiple_of(pp * ROWS, 16), ROWS), c0 : c0 + cw] = total.astype(jnp.bfloat16)
            return carry

        lax.fori_loop(0, 4, step, 0)

    def finish(n):
        c0, cw = CHUNKS[n]
        there = out_hbm.at[0, :, quarter(p, c0, cw)]

        def step(i, carry):
            to = ahead(p, dist(i))
            part = pl.ds(pl.multiple_of(to * ROWS, 16), ROWS)
            remote(T.at[part, pl.ds(c0, cw)], there, f_s, f_r, place(h, to, q)).start()
            return carry

        lax.fori_loop(0, 3, step, 0)
        part = pl.ds(pl.multiple_of(p * ROWS, 16), ROWS)
        mine = pltpu.make_async_copy(T.at[part, pl.ds(c0, cw)], there, own_sem.at[4 + n])
        mine.start()
        own.append(mine)

    def reduce_side(n):
        arrive(sums_in[n, 0])
        side_sum(n, h, 0, T)
        finish(n)

    def reduce_far_plane(n):
        arrive(sums_in[n, 0])
        side_sum(n, 1 - h, 0, T2)
        c0, cw = CHUNKS[n]
        cols = pl.ds(c0, cw)
        copy = remote(T2.at[:, cols], TY.at[:, cols], d_s.at[n], d_r.at[n], over)
        copy.start()
        back_in[n] = copy
        sent.append(copy)

    def reduce_own_plane(n):
        arrive(sums_in[n, 1])
        side_sum(n, h, 4, T)

    def reduce_last(n):
        c0, cw = CHUNKS[n]
        back_in[n].wait_recv()

        def step(pp, carry):
            part = pl.ds(pl.multiple_of(pp * ROWS, 16), ROWS)
            total = T[part, c0 : c0 + cw].astype(jnp.float32) + TY[part, c0 : c0 + cw].astype(jnp.float32)
            T[part, c0 : c0 + cw] = total.astype(jnp.bfloat16)
            return carry

        lax.fori_loop(0, 4, step, 0)
        finish(n)

    late = {"compute": compute, "over": reduce_over, "side": reduce_side, "last": reduce_last}
    late.update({"drain": drain, "far_plane": reduce_far_plane, "own_plane": reduce_own_plane})
    late.update(early)
    for name, *which in LATE:
        late[name](*which)
    total = T.at[pl.ds(0, 3 * len(CHUNKS) * ROWS * WIDE // COLS)]
    all_f = remote(total, total, f_s, f_r, near[0])
    all_f.wait_recv()
    units = 12 * ROWS * WIDE // COLS
    total = W.at[pl.ds(0, units * (len(CHUNKS) + len(W_OVER_FIRST)))]
    all_b = remote(total, total, b_s, f_r, near[0])
    total = W.at[pl.ds(0, units * (len(CHUNKS) + len(G_OVER_LAST)))]
    all_e = remote(total, total, e_s, f_r, near[0])
    sent.extend([all_f, all_b, all_e, remote(U, U, u_s, f_r, near[0])])
    drain()


def local(inputs, token_ids, upstream, weight, frag_index, global_params, local_params, momentum):
    n = len(CHUNKS)
    bf16, f32 = jnp.bfloat16, jnp.float32
    dma = pltpu.SemaphoreType.DMA
    sems = [dma((4,)), dma((3,)), dma((3,)), dma((4 + 2 * n,))]
    for send, receive in (
        ((2, 3), (2, 3)), ((3,), (3,)), ((4,), (4,)), ((), (n, 4)), ((), (n, 4)), ((n,), (n,)), ((n,), (n,)),
        ((), (n, 6)), ((), ()), ((n,), (n,)), ((n, 3), (n, 3)),
    ):
        sems += [dma(send), dma(receive)]
    sems.append(dma((n, 2)))
    hbm = pl.BlockSpec(memory_space=pltpu.HBM)
    span = global_params.shape[1]
    weight_grad, new_global, new_momentum = pl.pallas_call(
        kernel,
        name="inner_grad_outer_update",
        out_shape=(
            jax.ShapeDtypeStruct((1, ROWS, FW), bf16),
            jax.ShapeDtypeStruct((512, 128), f32),
            jax.ShapeDtypeStruct((512, 128), f32),
        ),
        in_specs=[hbm, hbm, hbm, hbm, pl.BlockSpec(memory_space=pltpu.SMEM), hbm, hbm, hbm],
        out_specs=[pl.BlockSpec(memory_space=pl.ANY)] * 3,
        scratch_shapes=[
            pltpu.VMEM((4, TOK, DW), bf16),
            pltpu.VMEM((DW, 4 * TOK), bf16),
            pltpu.VMEM((4 * TOK, COLS), bf16),
            pltpu.VMEM((DW, COLS), bf16),
            pltpu.VMEM((2, 4, 4, ROWS, COLS), bf16),
            pltpu.VMEM((4, 4, ROWS, COLS), bf16),
            pltpu.VMEM((3, 8, ROWS, COLS), bf16),
            pltpu.VMEM((4 * ROWS, COLS), bf16),
            pltpu.VMEM((4 * ROWS, COLS), bf16),
            pltpu.VMEM((4 * ROWS, COLS), bf16),
            pltpu.VMEM((4, ROWS, COLS), bf16),
            pltpu.VMEM((2, n, 256, WIDE), bf16),
            pltpu.VMEM((4, 8, TOK), f32),
            pltpu.VMEM((1, TOK), jnp.int32),
            pltpu.VMEM((16, span), f32),
            pltpu.VMEM((16, span), f32),
            pltpu.VMEM((16, span), f32),
            pltpu.VMEM((512, 128), f32),
            pltpu.VMEM((512, 128), f32),
            pltpu.VMEM((512, 128), bf16),
            pltpu.VMEM((256, 128), bf16),
            pltpu.VMEM((256, 128), bf16),
            pltpu.VMEM((256, 128), bf16),
            pltpu.VMEM((512, 128), f32),
            pltpu.VMEM((512, 128), f32),
            pltpu.VMEM((512, 128), f32),
            *sems,
        ],
        compiler_params=pltpu.CompilerParams(
            collective_id=0, has_side_effects=True, vmem_limit_bytes=int(52.75 * 2**20)
        ),
        cost_estimate=pl.CostEstimate(
            flops=4 * TOK * DW * FW, bytes_accessed=22 * 2**20, transcendentals=TOK * FW
        ),
    )(inputs, token_ids, upstream, weight, frag_index, global_params, local_params, momentum)
    return (weight_grad, new_global.reshape(span), new_momentum.reshape(span))


def solution(mesh):
    placed = (
        P("replica", "fsdp", None),
        P("replica", "fsdp"),
        P("replica", "fsdp", None),
        P("replica", "fsdp", None),
        P(),
        P(None, "fsdp"),
        P("replica", None, "fsdp"),
        P(None, "fsdp"),
    )
    return jax.shard_map(
        local,
        mesh=mesh,
        in_specs=placed,
        out_specs=(P("replica", "fsdp", None), P("fsdp"), P("fsdp")),
        check_vma=False,
    )
```
